1024 devices in a mesh: expert: 16 (over x, core), fsdp: 64 (over y, z).
Axes of the slice: x: 8, y: 8, z: 8, core: 2. Of those that a mesh axis runs over, the one named last changes fastest.
Arguments:
- tokens: bfloat16 [2048, 4096], P('fsdp', 'expert'), may hold values from -6 to 6
- input_weight: bfloat16 [64, 4096, 1536], P('fsdp', 'expert'), may hold values from -0.09375 to 0.09375
- output_weight: bfloat16 [64, 768, 4096], P('fsdp', None, 'expert'), may hold values from -0.21875 to 0.21875
- routes: int32 [2048, 8], P('fsdp'), may hold values from 0 to 63, all different within a row; in each aligned block of 32 rows (0 to 31, 32 to 63, ...) at most 8 rows name the same one
- gates: float32 [2048, 8], P('fsdp'), may hold values from 0.05 to 1
- cotangent: bfloat16 [2048, 4096], P('fsdp', 'expert'), may hold values from -6 to 6
Outputs:
- mixed: bfloat16 [2048, 4096], P('fsdp', 'expert')
- grad_tokens: bfloat16 [2048, 4096], P('fsdp', 'expert')
- grad_input: bfloat16 [64, 4096, 1536], P('fsdp', 'expert')
- grad_output: bfloat16 [64, 768, 4096], P('fsdp', None, 'expert')
The draws below stay inside these ranges and needn't reach their ends.
Inputs may be any that keep to these rules, and one draw needn't show every extreme that they name: `routes`: each token names 8 different experts. Among the tokens of one aligned block of 32 rows no expert is named more than 8 times, and in some block some expert is named exactly 8 times.
All inputs are finite; a program needn't handle non-finite values.
Results may differ from the reference program's by a relative error of at most 0.0064.
Values may be sent and summed in bfloat16 or wider, within the bound.
No kernel may reach another device: no remote copies, remote signals or barrier semaphores. Data moves between devices by JAX's collectives and lax.ppermute only.
A program may use at most 32 MiB of HBM per device.

```python
import math
import jax
import jax.numpy as jnp
import numpy as np
from jax import lax

D = 4096
TOP = 8
FF = 768
EXPERTS = 64
GROUP_TOK = 32
RECV = 8
TOKENS = 2048


def shard_levels(key, dims, shards, smallest, top_value):
    level = 1.0
    for axis_at, parts in shards:
        steps = jax.random.uniform(jax.random.fold_in(jax.random.fold_in(key, 6), axis_at), (parts,), jnp.float32, smallest / len(shards), top_value / len(shards))
        level = level * jnp.repeat(jnp.exp(steps), dims[axis_at] // parts).reshape((-1,) + (1,) * (len(dims) - 1 - axis_at))
    return level


def deal_out(own_key, own, number, rows, amount, top, limit, skew):
    order = jax.random.permutation(own_key, amount)
    heavy_load, usual = shares(amount, rows * top, limit, skew, True), shares(amount, rows * top, limit, skew, False)
    places = jnp.arange(amount)

    def named(sizes, rotation):
        used = int((sizes > 0).sum())
        fixed = max(1, used // 4)
        moved = fixed + (places - fixed + rotation * (used - fixed)) % max(1, amount - fixed)
        return jnp.zeros((amount,), jnp.int32).at[order[jnp.where(places < fixed, places, moved)]].set(jnp.asarray(sizes, jnp.int32))

    sizes = jnp.where(number % 4 == 0, named(heavy_load, number // 4), named(usual, number - number // 4 - 1))
    mixed = jax.random.permutation(jax.random.fold_in(own, 3), amount)
    donor, receiver = mixed[0:amount // 2 * 2:2], mixed[1:amount // 2 * 2:2]
    room = jnp.minimum(sizes[donor] - 1, limit - sizes[receiver]) // 2
    room = jnp.where((donor == order[0]) | (receiver == order[0]) | (sizes[receiver] == 0), 0, jnp.maximum(room, 0))
    moved = jax.random.randint(jax.random.fold_in(own, 4), (amount // 2,), 0, 1 << 20) % (room + 1)
    sizes = sizes.at[donor].add(-moved).at[receiver].add(moved)
    items = jnp.searchsorted(jnp.cumsum(sizes), jnp.arange(rows * top), side="right").astype(jnp.int32)
    grid = items.reshape(top, rows).T
    grid = grid[jax.random.permutation(jax.random.fold_in(own, 1), rows)]
    rotation = jax.random.randint(jax.random.fold_in(own, 2), (rows, 1), 0, top)
    return jnp.take_along_axis(grid, (jnp.arange(top)[None, :] + rotation) % top, axis=1)


def shares(number_of, total, reach, skew, full):
    loads = [(1 << 20) // math.isqrt(standing ** skew) + 1 for standing in range(1, number_of + 1)]
    largest = reach if full else min(reach, max(-(-total // number_of), total * loads[0] // sum(loads)))
    least = 1 if total - largest >= number_of - 1 else 0
    counts, spare = [largest] + [least] * (number_of - 1), total - largest - least * (number_of - 1)
    while spare > 0:
        free = [i for i in range(1, number_of) if counts[i] < largest] or [i for i in range(1, number_of) if counts[i] < reach]
        pool, remaining = sum([loads[i] for i in free]), spare
        for i in free:
            more = min(reach - counts[i], max(1, remaining * loads[i] // pool), spare)
            counts[i] = counts[i] + more
            spare = spare - more
    return np.array(counts)


def gaussian(key, extent, width, limit, cuts=(), kind=jnp.bfloat16):
    values = width * jax.random.normal(key, extent, jnp.float32)
    if cuts:
        values = values * shard_levels(key, extent, cuts, -0.22, 0.18)
    return jnp.clip(values, -limit, limit).astype(kind)


def setup_inputs(seed: int = 0) -> dict:
    arg_keys = jax.random.split(jax.random.key(seed), 7)
    tokens = gaussian(arg_keys[0], (TOKENS, D), 1.0, 6.0, ((0, 64), (1, 16)))
    input_weight = gaussian(arg_keys[1], (EXPERTS, D, 2 * FF), D ** -0.5, 0.09375, ((0, 64), (1, 16)))
    output_weight = gaussian(arg_keys[2], (EXPERTS, FF, D), FF ** -0.5, 0.21875, ((0, 64), (2, 16)))
    routes_keys = jax.random.split(jax.random.fold_in(arg_keys[3], 1), TOKENS // GROUP_TOK)
    routes_turns = jax.random.permutation(jax.random.fold_in(arg_keys[3], 3), TOKENS // GROUP_TOK)
    routes = jax.vmap(lambda own, number: deal_out(jax.random.fold_in(arg_keys[3], 2), own, number, GROUP_TOK, EXPERTS, TOP, RECV, 2))(routes_keys, routes_turns).reshape((TOKENS, TOP))
    gates = jnp.clip(jnp.exp(math.log(1.0) - 2.9957323 * jax.random.uniform(arg_keys[4], (TOKENS, TOP), jnp.float32) ** shard_levels(arg_keys[4], (TOKENS, TOP), ((0, 64),), -0.2, 0.2)), 0.05, 1.0)
    cotangent = gaussian(arg_keys[5], (TOKENS, D), 1.0, 6.0, ((0, 64), (1, 16)))
    return {"tokens": tokens, "input_weight": input_weight, "output_weight": output_weight, "routes": routes, "gates": gates, "cotangent": cotangent}


def swish_terms(pre_act, hidden_units):
    gate_part = pre_act[:, :hidden_units]
    up_part = pre_act[:, hidden_units:]
    sigma = jax.nn.sigmoid(gate_part)
    activated = gate_part * sigma
    return gate_part, up_part, sigma, activated


def backward_pre(back_hidden, gate_part, up_part, sigma, activated):
    slope = sigma + gate_part * sigma * (1.0 - sigma)
    grad_gate = back_hidden * up_part * slope
    grad_up = back_hidden * activated
    return jnp.concatenate([grad_gate, grad_up], axis=1).astype(jnp.bfloat16)


def reference(tokens, input_weight, output_weight, routes, gates, cotangent):
    token_count, model_width = tokens.shape
    route_count = routes.shape[1]
    hidden_units = output_weight.shape[1]
    blocks = token_count // GROUP_TOK
    per_block = GROUP_TOK * route_count
    table_rows = blocks * RECV
    block_routes = routes.reshape(blocks, per_block)
    onehot = (block_routes[:, :, None] == jnp.arange(EXPERTS, dtype=jnp.int32)[None, None, :]).astype(jnp.int32)
    earlier = jnp.cumsum(onehot, axis=1) - onehot
    slot_index = jnp.sum(earlier * onehot, axis=2).astype(jnp.int32)
    position = (jnp.arange(blocks, dtype=jnp.int32)[:, None] * RECV + slot_index).reshape(-1).astype(jnp.int32)
    expert_of = routes.reshape(-1).astype(jnp.int32)
    token_of = (jnp.arange(token_count * route_count, dtype=jnp.int32) // route_count).astype(jnp.int32)
    token_table = jnp.full((EXPERTS, table_rows), token_count, jnp.int32).at[expert_of, position].set(token_of)
    gate_table = jnp.zeros((EXPERTS, table_rows), jnp.float32).at[expert_of, position].set(gates.reshape(-1))
    padded_tokens = jnp.concatenate([tokens, jnp.zeros((1, model_width), tokens.dtype)], axis=0)
    padded_cotangent = jnp.concatenate([cotangent, jnp.zeros((1, model_width), cotangent.dtype)], axis=0)

    def per_expert(carry, inputs):
        mixed_sum, grad_sum = carry
        index_row, gate_values, weight_in, weight_out = inputs
        routed_rows = padded_tokens[index_row]
        routed_back = (gate_values[:, None] * padded_cotangent[index_row].astype(jnp.float32)).astype(jnp.bfloat16)
        pre_act = jnp.dot(routed_rows, weight_in, preferred_element_type=jnp.float32)
        gate_part, up_part, sigma, activated = swish_terms(pre_act, hidden_units)
        hidden = (activated * up_part).astype(jnp.bfloat16)
        expert_out = jnp.dot(hidden, weight_out, preferred_element_type=jnp.float32).astype(jnp.bfloat16)
        back_hidden = jnp.dot(routed_back, weight_out.T, preferred_element_type=jnp.float32)
        grad_pre = backward_pre(back_hidden, gate_part, up_part, sigma, activated)
        route_grad = jnp.dot(grad_pre, weight_in.T, preferred_element_type=jnp.float32).astype(jnp.bfloat16)
        mixed_sum = mixed_sum.at[index_row].add(gate_values[:, None] * expert_out.astype(jnp.float32))
        grad_sum = grad_sum.at[index_row].add(route_grad.astype(jnp.float32))
        grad_in = jnp.dot(routed_rows.T, grad_pre, preferred_element_type=jnp.float32).astype(jnp.bfloat16)
        grad_out = jnp.dot(hidden.T, routed_back, preferred_element_type=jnp.float32).astype(jnp.bfloat16)
        return (mixed_sum, grad_sum), (grad_in, grad_out)

    start_sums = (jnp.zeros((token_count + 1, model_width), jnp.float32), jnp.zeros((token_count + 1, model_width), jnp.float32))
    final_sums, stacked = lax.scan(per_expert, start_sums, (token_table, gate_table, input_weight, output_weight))
    mixed = final_sums[0][:token_count].astype(jnp.bfloat16)
    grad_tokens = final_sums[1][:token_count].astype(jnp.bfloat16)
    return mixed, grad_tokens, stacked[0], stacked[1]
```

```python
import jax
import jax.numpy as jnp
from jax import lax
from jax.sharding import PartitionSpec as P

LAST = (((1,), (1,)), ((), ()))
FIRST = (((0,), (0,)), ((), ()))


def dot(a, b, dims=(((1,), (0,)), ((), ()))):
    return lax.dot_general(a, b, dims, preferred_element_type=jnp.float32)


def swish_terms(pre_act, hidden_units):
    gate_part = pre_act[:, :hidden_units]
    up_part = pre_act[:, hidden_units:]
    sigma = jax.nn.sigmoid(gate_part)
    activated = gate_part * sigma
    return (gate_part, up_part, sigma, activated)


def local(tokens, input_weight, output_weight, routes, gates, cotangent):
    block_tok, width = tokens.shape
    route_count = routes.shape[1]
    experts = lax.axis_size("fsdp")
    ff = output_weight.shape[1]
    capacity = min(block_tok, 2 * block_tok * route_count // experts)
    rows = experts * capacity
    weight_in = input_weight[0]
    weight_out = output_weight[0]

    flat_routes = routes.reshape(-1)
    onehot = (flat_routes[:, None] == jnp.arange(experts, dtype=jnp.int32)[None, :]).astype(
        jnp.int32
    )
    earlier = jnp.cumsum(onehot, axis=0) - onehot
    slot_index = jnp.sum(earlier * onehot, axis=1).reshape(block_tok, route_count)
    target = routes * capacity + slot_index
    hit = target[:, :, None] == jnp.arange(rows, dtype=jnp.int32)[None, None, :]
    picker = jnp.any(hit, axis=1).astype(jnp.bfloat16)
    gate_map = jnp.sum(jnp.where(hit, gates[:, :, None], 0.0), axis=1)
    slot_gate = jnp.sum(gate_map, axis=0)
    send_rows = dot(picker, tokens, FIRST).astype(jnp.bfloat16)
    send_back = (slot_gate[:, None] * dot(picker, cotangent, FIRST)).astype(jnp.bfloat16)
    sent = jnp.concatenate(
        [send_rows.reshape(experts, capacity, width), send_back.reshape(experts, capacity, width)],
        axis=1,
    )
    got = lax.all_to_all(sent, "fsdp", split_axis=0, concat_axis=0, tiled=True)
    routed_rows = got[:, :capacity].reshape(rows, width)
    routed_back = got[:, capacity:].reshape(rows, width)

    chips = lax.axis_size("expert") // 2
    device = lax.axis_index("expert")
    piece = rows // (2 * chips)
    core = device & 1

    def half(values, which):
        pieces = values.reshape(chips, 2, piece, width)
        return lax.dynamic_index_in_dim(pieces, which, 1, keepdims=False).reshape(-1, width)

    def partial_sums(which):
        return jnp.concatenate(
            [
                dot(half(routed_rows, which), weight_in),
                dot(half(routed_back, which), weight_out, LAST),
            ],
            axis=1,
        )

    swap = [(d, d ^ 1) for d in range(2 * chips)]
    same_core = [[2 * i + c for i in range(chips)] for c in range(2)]
    arrived = lax.ppermute(partial_sums(1 - core).astype(jnp.bfloat16), "expert", swap)
    chip_sum = (partial_sums(core) + arrived.astype(jnp.float32)).astype(jnp.bfloat16)
    pieces = lax.all_to_all(
        chip_sum.reshape(chips, piece, 3 * ff),
        "expert",
        split_axis=0,
        concat_axis=0,
        tiled=True,
        axis_index_groups=same_core,
    )
    share = jnp.sum(pieces.astype(jnp.float32), axis=0)
    gate_part, up_part, sigma, activated = swish_terms(share[:, : 2 * ff], ff)
    back_hidden = share[:, 2 * ff :]
    slope = sigma + gate_part * sigma * (1.0 - sigma)
    hidden, grad_gate, grad_up = (
        lax.all_gather(part.astype(jnp.bfloat16), "expert", axis=0, tiled=True)
        for part in (activated * up_part, back_hidden * up_part * slope, back_hidden * activated)
    )
    grad_pre = jnp.concatenate([grad_gate, grad_up], axis=1)

    out_rows = dot(hidden, weight_out).astype(jnp.bfloat16)
    route_grad = dot(grad_pre, weight_in, LAST).astype(jnp.bfloat16)
    back = jnp.concatenate(
        [out_rows.reshape(experts, capacity, width), route_grad.reshape(experts, capacity, width)],
        axis=1,
    )
    home = lax.all_to_all(back, "fsdp", split_axis=0, concat_axis=0, tiled=True)
    grad_input = dot(routed_rows, grad_pre, FIRST).astype(jnp.bfloat16)[None]
    grad_output = dot(hidden, routed_back, FIRST).astype(jnp.bfloat16)[None]
    mixed = lax.dot(
        gate_map,
        home[:, :capacity].reshape(rows, width).astype(jnp.float32),
        precision=lax.Precision.HIGHEST,
    ).astype(jnp.bfloat16)
    grad_tokens = dot(picker, home[:, capacity:].reshape(rows, width)).astype(jnp.bfloat16)
    return (mixed, grad_tokens, grad_input, grad_output)


def solution(mesh):
    placed = (
        P("fsdp", "expert"),
        P("fsdp", "expert", None),
        P("fsdp", None, "expert"),
        P("fsdp", None),
        P("fsdp", None),
        P("fsdp", "expert"),
    )
    return jax.shard_map(
        local,
        mesh=mesh,
        in_specs=placed,
        out_specs=(
            P("fsdp", "expert"),
            P("fsdp", "expert"),
            P("fsdp", "expert", None),
            P("fsdp", None, "expert"),
        ),
        check_vma=False,
    )
```

```python
import jax
import jax.numpy as jnp
from jax import lax
from jax.experimental import pallas as pl
from jax.experimental.pallas import tpu as pltpu
from jax.sharding import PartitionSpec as P

PLAIN = (((1,), (0,)), ((), ()))
LAST = (((1,), (1,)), ((), ()))
FIRST = (((0,), (0,)), ((), ()))


def dot(a, b, dims=PLAIN):
    return lax.dot_general(a, b, dims, preferred_element_type=jnp.float32)


def bf16_parts(values):
    first = values.astype(jnp.bfloat16)
    rest = values - first.astype(jnp.float32)
    second = rest.astype(jnp.bfloat16)
    third = (rest - second.astype(jnp.float32)).astype(jnp.bfloat16)
    return first, second, third


def dispatch_kernel(capacity, routes_ref, gates_ref, tokens_ref, cotangent_ref, sent_ref, maps_ref):
    experts, _, width = sent_ref.shape
    count, route_count = routes_ref.shape
    rows = experts * capacity
    routes = routes_ref[...]
    gates = gates_ref[...]
    lane = lax.broadcasted_iota(jnp.int32, (count, experts), 1)
    named = jnp.zeros((count, experts), jnp.float32)
    gate_of = jnp.zeros((count, experts), jnp.float32)
    for k in range(route_count):
        hit = routes[:, k : k + 1] == lane
        named = jnp.where(hit, 1.0, named)
        gate_of = jnp.where(hit, gates[:, k : k + 1], gate_of)
    row = lax.broadcasted_iota(jnp.int32, (count, count), 0)
    column = lax.broadcasted_iota(jnp.int32, (count, count), 1)
    before = jnp.where(column < row, 1.0, 0.0).astype(jnp.bfloat16)
    named = named.astype(jnp.bfloat16)
    slot = dot(before, named).astype(jnp.bfloat16)
    first_row = lax.broadcasted_iota(jnp.int32, (experts, rows), 0) * capacity
    at = lax.broadcasted_iota(jnp.int32, (experts, rows), 1)
    inside = (at >= first_row) & (at < first_row + capacity)
    spread = jnp.where(inside, 1.0, 0.0).astype(jnp.bfloat16)
    local_slot = jnp.sum(jnp.where(inside, at - first_row, 0), axis=0, keepdims=True)
    picked = (dot(named, spread) > 0.5) & (dot(slot, spread) == local_slot.astype(jnp.float32))
    picker = jnp.where(picked, 1.0, 0.0).astype(jnp.bfloat16)
    ones = jnp.ones((count, width), jnp.bfloat16)
    row_gate = jnp.zeros((rows, width), jnp.float32)
    for i, part in enumerate(bf16_parts(gate_of)):
        spread_part = jnp.where(picked, dot(part, spread), 0.0).astype(jnp.bfloat16)
        maps_ref[i * count : (i + 1) * count, :] = spread_part
        row_gate = row_gate + dot(spread_part, ones, FIRST)
    maps_ref[3 * count : 4 * count, :] = picker
    send_rows = dot(picker, tokens_ref[...], FIRST)
    send_back = row_gate * dot(picker, cotangent_ref[...], FIRST)
    sent_ref[...] = jnp.concatenate(
        [send_rows.reshape(experts, capacity, width), send_back.reshape(experts, capacity, width)],
        axis=1,
    ).astype(jnp.bfloat16)


def combine_kernel(capacity, maps_ref, home_ref, mixed_ref, grad_ref):
    experts, _, width = home_ref.shape
    count = mixed_ref.shape[0]
    rows = experts * capacity
    home = home_ref[...].astype(jnp.float32)
    out = home[:, :capacity, :].reshape(rows, width).astype(jnp.bfloat16)
    grad = home[:, capacity:, :].reshape(rows, width).astype(jnp.bfloat16)
    total = dot(maps_ref[0:count, :], out)
    total = total + dot(maps_ref[count : 2 * count, :], out)
    total = total + dot(maps_ref[2 * count : 3 * count, :], out)
    mixed_ref[...] = total.astype(jnp.bfloat16)
    grad_ref[...] = dot(maps_ref[3 * count : 4 * count, :], grad).astype(jnp.bfloat16)


def call(kernel, out_shape, flops, *operands):
    def size(a):
        return a.size * a.dtype.itemsize

    moved = sum(map(size, operands)) + sum(map(size, jax.tree.leaves(out_shape)))
    return pl.pallas_call(
        kernel,
        out_shape=out_shape,
        compiler_params=pltpu.CompilerParams(vmem_limit_bytes=40 * 2**20),
        cost_estimate=pl.CostEstimate(flops=flops, bytes_accessed=moved, transcendentals=0),
    )(*operands)


def local(tokens, input_weight, output_weight, routes, gates, cotangent):
    block_tok, width = tokens.shape
    route_count = routes.shape[1]
    experts = lax.axis_size("fsdp")
    chips = lax.axis_size("expert") // 2
    ff = output_weight.shape[1]
    capacity = min(block_tok, 2 * block_tok * route_count // experts)
    rows = experts * capacity
    piece = rows // (2 * chips)
    core = lax.axis_index("expert") & 1
    weight_in = input_weight[0]
    weight_out = output_weight[0]
    swap = [(d, d ^ 1) for d in range(2 * chips)]
    same_core = [[2 * i + c for i in range(chips)] for c in range(2)]

    def exchange(values):
        return lax.all_to_all(values, "fsdp", split_axis=0, concat_axis=0, tiled=True)

    def exchange_chips(values):
        return lax.all_to_all(
            values, "expert", split_axis=0, concat_axis=0, tiled=True, axis_index_groups=same_core
        )

    def half(values, which):
        pieces = values.reshape(chips, 2, piece, width)
        return lax.dynamic_index_in_dim(pieces, which, 1, keepdims=False).reshape(-1, width)

    def both(mine, other):
        mine = mine.reshape(chips, piece, -1)
        other = other.reshape(chips, piece, -1)
        first = core == 0
        return jnp.stack(
            [jnp.where(first, mine, other), jnp.where(first, other, mine)], axis=1
        ).reshape(rows, -1)

    sent, maps = call(
        lambda *refs: dispatch_kernel(capacity, *refs),
        (
            jax.ShapeDtypeStruct((experts, 2 * capacity, width), jnp.bfloat16),
            jax.ShapeDtypeStruct((4 * block_tok, rows), jnp.bfloat16),
        ),
        10 * rows * block_tok * width,
        routes,
        gates,
        tokens,
        cotangent,
    )
    got = exchange(sent)
    routed_rows = got[:, :capacity].reshape(rows, width)
    routed_back = got[:, capacity:].reshape(rows, width)
    mine_rows, other_rows = half(routed_rows, core), half(routed_rows, 1 - core)
    mine_back, other_back = half(routed_back, core), half(routed_back, 1 - core)

    def partial_sums(some_rows, some_back):
        return jnp.concatenate(
            [dot(some_rows, weight_in), dot(some_back, weight_out, LAST)], axis=1
        )

    arrived = lax.ppermute(
        partial_sums(other_rows, other_back).astype(jnp.bfloat16), "expert", swap
    )
    chip_sum = partial_sums(mine_rows, mine_back) + arrived.astype(jnp.float32)
    pieces = exchange_chips(chip_sum.astype(jnp.bfloat16).reshape(chips, piece, 3 * ff))
    share = jnp.sum(pieces.astype(jnp.float32), axis=0)
    gate_part, up_part, back_hidden = share[:, :ff], share[:, ff : 2 * ff], share[:, 2 * ff :]
    sigma = jax.nn.sigmoid(gate_part)
    activated = gate_part * sigma
    slope = sigma + gate_part * sigma * (1.0 - sigma)
    grad_share = jnp.concatenate(
        [back_hidden * up_part * slope, back_hidden * activated], axis=1
    ).astype(jnp.bfloat16)
    hidden_share = (activated * up_part).astype(jnp.bfloat16)

    mine_grad = exchange_chips(
        jnp.broadcast_to(grad_share[None], (chips, *grad_share.shape))
    ).reshape(-1, 2 * ff)
    hidden = lax.all_gather(hidden_share, "expert", axis=0, tiled=True)
    mine_grad, hidden = lax.optimization_barrier((mine_grad, hidden))
    other_grad = lax.ppermute(mine_grad, "expert", swap)
    out_rows = dot(hidden, weight_out).astype(jnp.bfloat16)
    route_grad = both(
        dot(mine_grad, weight_in, LAST).astype(jnp.bfloat16),
        dot(other_grad, weight_in, LAST).astype(jnp.bfloat16),
    )
    back = jnp.concatenate(
        [out_rows.reshape(experts, capacity, width), route_grad.reshape(experts, capacity, width)],
        axis=1,
    )
    home = exchange(back)
    grad_input = (
        (dot(mine_rows, mine_grad, FIRST) + dot(other_rows, other_grad, FIRST))
        .astype(jnp.bfloat16)
    )[None]
    grad_output = dot(hidden, routed_back, FIRST).astype(jnp.bfloat16)[None]
    mixed, grad_tokens = call(
        lambda *refs: combine_kernel(capacity, *refs),
        (
            jax.ShapeDtypeStruct((block_tok, width), jnp.bfloat16),
            jax.ShapeDtypeStruct((block_tok, width), jnp.bfloat16),
        ),
        8 * rows * block_tok * width,
        maps,
        home,
    )
    return (mixed, grad_tokens, grad_input, grad_output)


def solution(mesh):
    placed = (
        P("fsdp", "expert"),
        P("fsdp", "expert", None),
        P("fsdp", None, "expert"),
        P("fsdp", None),
        P("fsdp", None),
        P("fsdp", "expert"),
    )
    return jax.shard_map(
        local,
        mesh=mesh,
        in_specs=placed,
        out_specs=(
            P("fsdp", "expert"),
            P("fsdp", "expert"),
            P("fsdp", "expert", None),
            P("fsdp", None, "expert"),
        ),
        check_vma=False,
    )
```

```python
import jax
import jax.numpy as jnp
from jax import lax
from jax.experimental import pallas as pl
from jax.experimental.pallas import tpu as pltpu
from jax.sharding import PartitionSpec as P

PLAIN = (((1,), (0,)), ((), ()))
LAST = (((1,), (1,)), ((), ()))
FIRST = (((0,), (0,)), ((), ()))
UNIT = 32


def dot(a, b, dims=PLAIN):
    return lax.dot_general(a, b, dims, preferred_element_type=jnp.float32)


def bf16_parts(values):
    first = values.astype(jnp.bfloat16)
    rest = values - first.astype(jnp.float32)
    second = rest.astype(jnp.bfloat16)
    third = (rest - second.astype(jnp.float32)).astype(jnp.bfloat16)
    return first, second, third


def dispatch_kernel(capacity, routes_ref, gates_ref, tokens_ref, cotangent_ref, sent_ref, maps_ref):
    experts, _, width = sent_ref.shape
    count, route_count = routes_ref.shape
    rows = experts * capacity
    routes = routes_ref[...]
    gates = gates_ref[...]
    lane = lax.broadcasted_iota(jnp.int32, (count, experts), 1)
    named = jnp.zeros((count, experts), jnp.float32)
    gate_of = jnp.zeros((count, experts), jnp.float32)
    for k in range(route_count):
        hit = routes[:, k : k + 1] == lane
        named = jnp.where(hit, 1.0, named)
        gate_of = jnp.where(hit, gates[:, k : k + 1], gate_of)
    row = lax.broadcasted_iota(jnp.int32, (count, count), 0)
    column = lax.broadcasted_iota(jnp.int32, (count, count), 1)
    before = jnp.where(column < row, 1.0, 0.0).astype(jnp.bfloat16)
    named = named.astype(jnp.bfloat16)
    slot = dot(before, named).astype(jnp.bfloat16)
    first_row = lax.broadcasted_iota(jnp.int32, (experts, rows), 0) * capacity
    at = lax.broadcasted_iota(jnp.int32, (experts, rows), 1)
    inside = (at >= first_row) & (at < first_row + capacity)
    spread = jnp.where(inside, 1.0, 0.0).astype(jnp.bfloat16)
    local_slot = jnp.sum(jnp.where(inside, at - first_row, 0), axis=0, keepdims=True)
    picked = (dot(named, spread) > 0.5) & (dot(slot, spread) == local_slot.astype(jnp.float32))
    picker = jnp.where(picked, 1.0, 0.0).astype(jnp.bfloat16)
    ones = jnp.ones((count, width), jnp.bfloat16)
    row_gate = jnp.zeros((rows, width), jnp.float32)
    for i, part in enumerate(bf16_parts(gate_of)):
        spread_part = jnp.where(picked, dot(part, spread), 0.0).astype(jnp.bfloat16)
        maps_ref[i * count : (i + 1) * count, :] = spread_part
        row_gate = row_gate + dot(spread_part, ones, FIRST)
    maps_ref[3 * count : 4 * count, :] = picker
    send_rows = dot(picker, tokens_ref[...], FIRST)
    send_back = row_gate * dot(picker, cotangent_ref[...], FIRST)
    sent_ref[...] = jnp.concatenate(
        [send_rows.reshape(experts, capacity, width), send_back.reshape(experts, capacity, width)],
        axis=1,
    ).astype(jnp.bfloat16)


def combine_kernel(capacity, maps_ref, home_ref, mixed_ref, grad_ref):
    experts, _, width = home_ref.shape
    count = mixed_ref.shape[0]
    rows = experts * capacity
    home = home_ref[...].astype(jnp.float32)
    out = home[:, :capacity, :].reshape(rows, width).astype(jnp.bfloat16)
    grad = home[:, capacity:, :].reshape(rows, width).astype(jnp.bfloat16)
    total = dot(maps_ref[0:count, :], out)
    total = total + dot(maps_ref[count : 2 * count, :], out)
    total = total + dot(maps_ref[2 * count : 3 * count, :], out)
    mixed_ref[...] = total.astype(jnp.bfloat16)
    grad_ref[...] = dot(maps_ref[3 * count : 4 * count, :], grad).astype(jnp.bfloat16)


def unit_order(me, chips):
    chip, core = lax.div(me, 2), lax.rem(me, 2)
    sign, twin = 1 - 2 * core, 1 - core
    opposite = 2 * lax.rem(chip + 4, chips)
    order = [2 * chip + twin]
    for distance in (1, 2, 3):
        at = 2 * lax.rem(chip - sign * distance + chips, chips)
        order += [at + core, at + twin]
    order += [2 * chip + core, opposite + core]
    for distance in (1, 2, 3):
        at = 2 * lax.rem(chip + sign * distance + chips, chips)
        order += [at + twin, at + core]
    return order + [opposite + twin]


def sums_kernel(capacity, me_ref, got_ref, twin_got_ref, in_ref, twin_in_ref, out_ref, twin_out_ref,
                rows_ref, back_ref, own_ref, far_ref, near_ref, middle_ref, third_ref,
                twin_rows, twin_back):
    experts, _, width = got_ref.shape
    units = rows_ref.shape[0] // UNIT
    blocks = UNIT // capacity
    for k, unit in enumerate(unit_order(me_ref[0], units // 2)):
        here = slice(k * UNIT, (k + 1) * UNIT)
        for source, row_to, back_to in (
            (got_ref, rows_ref, back_ref),
            (twin_got_ref, twin_rows, twin_back),
        ):
            block = source[pl.ds(unit * blocks, blocks)].astype(jnp.float32)
            row_to[here, :] = block[:, :capacity].reshape(UNIT, width).astype(jnp.bfloat16)
            back_to[here, :] = block[:, capacity:].reshape(UNIT, width).astype(jnp.bfloat16)
    part = slice(7 * UNIT, 15 * UNIT)
    ff = out_ref.shape[0]

    def put(columns, total):
        own_ref[:, columns] = total[:UNIT]
        far_ref[:, columns] = total[UNIT : 2 * UNIT].astype(jnp.bfloat16)
        near_ref[:, columns] = total[2 * UNIT : 4 * UNIT].astype(jnp.bfloat16)
        middle_ref[:, columns] = total[4 * UNIT : 6 * UNIT]
        third_ref[:, columns] = total[6 * UNIT :].astype(jnp.bfloat16)

    step = ff // 2
    for start in range(0, 2 * ff, step):
        columns = slice(start, start + step)
        put(
            columns,
            dot(rows_ref[part, :], in_ref[:, columns]) + dot(twin_rows[part, :], twin_in_ref[:, columns]),
        )
    for start in range(0, ff, step):
        some = slice(start, start + step)
        put(
            slice(2 * ff + start, 2 * ff + start + step),
            dot(back_ref[part, :], out_ref[some, :], LAST)
            + dot(twin_back[part, :], twin_out_ref[some, :], LAST),
        )


def gateway_kernel(middle_ref, third_ref, far_ref, sum_ref):
    total = middle_ref[...] + third_ref[...].astype(jnp.float32)
    sum_ref[:UNIT, :] = total[:UNIT].astype(jnp.bfloat16)
    sum_ref[UNIT:, :] = (total[UNIT:] + far_ref[...].astype(jnp.float32)).astype(jnp.bfloat16)


def twin_part_kernel(near_ref, passed_ref, sum_ref):
    sum_ref[...] = near_ref[:UNIT, :].astype(jnp.float32) + passed_ref[:UNIT, :].astype(jnp.float32)


def swish_kernel(own_ref, near_ref, passed_ref, twin_ref, mid_ref):
    share = (
        own_ref[...]
        + near_ref[UNIT:, :].astype(jnp.float32)
        + passed_ref[UNIT:, :].astype(jnp.float32)
        + twin_ref[...]
    )
    ff = share.shape[1] // 3
    gate_part, up_part, back_hidden = share[:, :ff], share[:, ff : 2 * ff], share[:, 2 * ff :]
    sigma = jax.nn.sigmoid(gate_part)
    activated = gate_part * sigma
    slope = sigma + gate_part * sigma * (1.0 - sigma)
    mid_ref[:, :ff] = (activated * up_part).astype(jnp.bfloat16)
    mid_ref[:, ff : 2 * ff] = (back_hidden * up_part * slope).astype(jnp.bfloat16)
    mid_ref[:, 2 * ff :] = (back_hidden * activated).astype(jnp.bfloat16)


def results_kernel(capacity, me_ref, in_ref, out_ref, *refs):
    parts, (back_ref, full_ref) = refs[:-2], refs[-2:]
    at = 0
    for part in parts:
        count = part.shape[0]
        full_ref[at : at + count, :] = part[...]
        at += count
    ff, width = out_ref.shape
    out = dot(full_ref[:, :ff], out_ref[...])
    grad = dot(full_ref[:, ff:], in_ref[...], LAST)
    units = full_ref.shape[0] // UNIT
    blocks = UNIT // capacity
    for k, unit in enumerate(unit_order(me_ref[0], units // 2)):
        here = slice(k * UNIT, (k + 1) * UNIT)
        back_ref[pl.ds(unit * blocks, blocks)] = jnp.concatenate(
            [
                out[here].reshape(blocks, capacity, width),
                grad[here].reshape(blocks, capacity, width),
            ],
            axis=1,
        ).astype(jnp.bfloat16)


def call(kernel, out_shape, flops, *operands, scratch=(), scalar_first=False):
    def size(a):
        return a.size * a.dtype.itemsize

    moved = sum(map(size, operands)) + sum(map(size, jax.tree.leaves(out_shape)))
    specs = [pl.BlockSpec(memory_space=pltpu.VMEM) for _ in operands]
    if scalar_first:
        specs[0] = pl.BlockSpec(memory_space=pltpu.SMEM)
    return pl.pallas_call(
        kernel,
        out_shape=out_shape,
        in_specs=specs,
        scratch_shapes=scratch,
        compiler_params=pltpu.CompilerParams(vmem_limit_bytes=40 * 2**20),
        cost_estimate=pl.CostEstimate(flops=flops, bytes_accessed=moved, transcendentals=0),
    )(*operands)


def local(tokens, input_weight, output_weight, routes, gates, cotangent):
    block_tok, width = tokens.shape
    route_count = routes.shape[1]
    experts = lax.axis_size("fsdp")
    chips = lax.axis_size("expert") // 2
    ff = output_weight.shape[1]
    capacity = min(block_tok, 2 * block_tok * route_count // experts)
    rows = experts * capacity
    weight_in = input_weight[0]
    weight_out = output_weight[0]
    me = lax.axis_index("expert").reshape(1)
    bf16, f32 = jnp.bfloat16, jnp.float32

    def exchange(values):
        return lax.all_to_all(values, "fsdp", split_axis=0, concat_axis=0, tiled=True)

    def swap(values):
        return lax.ppermute(values, "expert", [(d, d ^ 1) for d in range(2 * chips)])

    def along(values, distance):
        up = [(2 * i, 2 * ((i + distance) % chips)) for i in range(chips)]
        down = [(2 * i + 1, 2 * ((i - distance) % chips) + 1) for i in range(chips)]
        return lax.ppermute(values, "expert", up + down)

    def array(count, columns, dtype):
        return jax.ShapeDtypeStruct((count, columns), dtype)

    sent, maps = call(
        lambda *refs: dispatch_kernel(capacity, *refs),
        (
            jax.ShapeDtypeStruct((experts, 2 * capacity, width), jnp.bfloat16),
            jax.ShapeDtypeStruct((4 * block_tok, rows), jnp.bfloat16),
        ),
        10 * rows * block_tok * width,
        routes,
        gates,
        tokens,
        cotangent,
    )
    sent, *ready = lax.optimization_barrier((sent, weight_in, weight_out))
    got, twin_in, twin_out = lax.optimization_barrier((exchange(sent), *map(swap, ready)))
    all_columns = 3 * ff
    routed_rows, routed_back, own, far, near, middle, third = call(
        lambda *refs: sums_kernel(capacity, *refs),
        (
            array(rows, width, bf16),
            array(rows, width, bf16),
            array(UNIT, all_columns, f32),
            array(UNIT, all_columns, bf16),
            array(2 * UNIT, all_columns, bf16),
            array(2 * UNIT, all_columns, f32),
            array(2 * UNIT, all_columns, bf16),
        ),
        4 * 8 * UNIT * width * all_columns,
        me,
        got,
        swap(got),
        weight_in,
        twin_in,
        weight_out,
        twin_out,
        scratch=[pltpu.VMEM((rows, width), bf16), pltpu.VMEM((rows, width), bf16)],
        scalar_first=True,
    )
    third = along(third, 1)
    far = along(far, 2)
    near = along(near, 1)
    passed = along(
        call(gateway_kernel, array(2 * UNIT, all_columns, bf16), rows * ff, middle, third, far), 2
    )
    twin_part = swap(call(twin_part_kernel, array(UNIT, all_columns, f32), rows * ff, near, passed))
    mid = call(
        swish_kernel, array(UNIT, all_columns, bf16), rows * ff, own, near, passed, twin_part
    )

    twin_mid = swap(mid)
    chip_mid = jnp.concatenate([mid, twin_mid], axis=0)
    second = along(chip_mid, 2)
    first = along(chip_mid, 1)
    third = along(second, 1)
    far = along(second[:UNIT], 2)
    back, full = call(
        lambda *refs: results_kernel(capacity, *refs),
        (
            jax.ShapeDtypeStruct((experts, 2 * capacity, width), bf16),
            array(rows, all_columns, bf16),
        ),
        2 * rows * width * all_columns,
        me,
        weight_in,
        weight_out,
        twin_mid,
        first,
        second,
        third,
        mid,
        far,
        swap(first),
        swap(second),
        swap(third),
        swap(far),
        scalar_first=True,
    )
    home = exchange(back)
    hidden, grad_pre = full[:, :ff], full[:, ff:]
    grad_input = dot(routed_rows, grad_pre, FIRST).astype(bf16)[None]
    grad_output = dot(hidden, routed_back, FIRST).astype(bf16)[None]
    mixed, grad_tokens = call(
        lambda *refs: combine_kernel(capacity, *refs),
        (
            jax.ShapeDtypeStruct((block_tok, width), jnp.bfloat16),
            jax.ShapeDtypeStruct((block_tok, width), jnp.bfloat16),
        ),
        8 * rows * block_tok * width,
        maps,
        home,
    )
    return (mixed, grad_tokens, grad_input, grad_output)


def solution(mesh):
    placed = (
        P("fsdp", "expert"),
        P("fsdp", "expert", None),
        P("fsdp", None, "expert"),
        P("fsdp", None),
        P("fsdp", None),
        P("fsdp", "expert"),
    )
    return jax.shard_map(
        local,
        mesh=mesh,
        in_specs=placed,
        out_specs=(
            P("fsdp", "expert"),
            P("fsdp", "expert"),
            P("fsdp", "expert", None),
            P("fsdp", None, "expert"),
        ),
        check_vma=False,
    )
```

```python
import jax
import jax.numpy as jnp
from jax import lax
from jax.experimental import pallas as pl
from jax.experimental.pallas import tpu as pltpu
from jax.sharding import PartitionSpec as P

PLAIN = (((1,), (0,)), ((), ()))
LAST = (((1,), (1,)), ((), ()))
FIRST = (((0,), (0,)), ((), ()))
UNIT = 32


def dot(a, b, dims=PLAIN):
    return lax.dot_general(a, b, dims, preferred_element_type=jnp.float32)


def bf16_parts(values):
    first = values.astype(jnp.bfloat16)
    rest = values - first.astype(jnp.float32)
    second = rest.astype(jnp.bfloat16)
    third = (rest - second.astype(jnp.float32)).astype(jnp.bfloat16)
    return first, second, third


def dispatch_kernel(capacity, routes_hbm, gates_hbm, tokens_hbm, cotangent_hbm, sent_ref, maps_ref,
                    routes_ref, gates_ref, tokens_ref, cotangent_ref, arrived):
    experts, _, width = sent_ref.shape
    rows, lanes = maps_ref.shape
    route_count, count = routes_hbm.shape
    copies = [
        pltpu.make_async_copy(source, target, arrived.at[i])
        for i, (source, target) in enumerate(
            (
                (routes_hbm, routes_ref),
                (gates_hbm, gates_ref),
                (tokens_hbm, tokens_ref.at[3 * count : 4 * count]),
                (cotangent_hbm, cotangent_ref.at[3 * count : 4 * count]),
            )
        )
    ]
    for copy in copies:
        copy.start()
    tokens_ref[: 3 * count, :] = jnp.zeros((3 * count, width), jnp.bfloat16)
    cotangent_ref[: 3 * count, :] = jnp.zeros((3 * count, width), jnp.bfloat16)
    token = lax.broadcasted_iota(jnp.int32, (count, lanes), 0)
    lane = lax.broadcasted_iota(jnp.int32, (count, lanes), 1)
    group = [lane == token + i * count for i in range(4)]
    group = [jnp.where(one, 1.0, 0.0).astype(jnp.bfloat16) for one in group]
    first_row = lax.broadcasted_iota(jnp.int32, (rows, experts), 1) * capacity
    at = lax.broadcasted_iota(jnp.int32, (rows, experts), 0)
    inside = (at >= first_row) & (at < first_row + capacity)
    spread = jnp.where(inside, 1.0, 0.0).astype(jnp.bfloat16)
    local_slot = jnp.sum(jnp.where(inside, at - first_row, 0), axis=1, keepdims=True)
    copies[0].wait()
    copies[1].wait()
    everywhere = group[0] + group[1] + group[2] + group[3]
    routes = dot(routes_ref[...].astype(jnp.float32).astype(jnp.bfloat16), everywhere)
    ones = jnp.ones((route_count, count), jnp.bfloat16)
    values = jnp.zeros((route_count, lanes), jnp.float32)
    for part, lanes_of in zip((*bf16_parts(gates_ref[...]), ones), group):
        values = values + dot(part, lanes_of)
    expert = lax.broadcasted_iota(jnp.int32, (experts, lanes), 0).astype(jnp.float32)
    named = jnp.zeros((experts, lanes), jnp.float32)
    value_of = jnp.zeros((experts, lanes), jnp.float32)
    for k in range(route_count):
        hit = routes[k : k + 1, :] == expert
        named = jnp.where(hit, 1.0, named)
        value_of = jnp.where(hit, values[k : k + 1, :], value_of)
    other = lax.broadcasted_iota(jnp.int32, (lanes, lanes), 0)
    mine = lax.broadcasted_iota(jnp.int32, (lanes, lanes), 1)
    for _ in range(3):
        mine = jnp.where(mine >= count, mine - count, mine)
    before = jnp.where(other < mine, 1.0, 0.0).astype(jnp.bfloat16)
    named = named.astype(jnp.bfloat16)
    slot = dot(named, before).astype(jnp.bfloat16)
    picked = (dot(spread, named) > 0.5) & (dot(spread, slot) == local_slot.astype(jnp.float32))
    maps = jnp.where(picked, dot(spread, value_of.astype(jnp.bfloat16)), 0.0)
    is_gate = lax.broadcasted_iota(jnp.int32, (rows, lanes), 1) < 3 * count
    row_gate = jnp.sum(jnp.where(is_gate, maps, 0.0), axis=1, keepdims=True)
    maps = maps.astype(jnp.bfloat16)
    maps_ref[...] = maps
    copies[2].wait()
    copies[3].wait()
    send_rows = dot(maps, tokens_ref[...])
    send_back = row_gate * dot(maps, cotangent_ref[...])
    sent_ref[...] = jnp.concatenate(
        [send_rows.reshape(experts, capacity, width), send_back.reshape(experts, capacity, width)],
        axis=1,
    ).astype(jnp.bfloat16)


def combine_kernel(capacity, maps_ref, home_ref, mixed_ref, grad_ref):
    experts, _, width = home_ref.shape
    count = mixed_ref.shape[0]
    rows = experts * capacity
    home = home_ref[...].astype(jnp.float32)
    out = home[:, :capacity, :].reshape(rows, width).astype(jnp.bfloat16)
    grad = home[:, capacity:, :].reshape(rows, width).astype(jnp.bfloat16)
    total = dot(maps_ref[...], out, FIRST)
    total = total[:count] + total[count : 2 * count] + total[2 * count : 3 * count]
    mixed_ref[...] = total.astype(jnp.bfloat16)
    grad_ref[...] = dot(maps_ref[...], grad, FIRST)[3 * count :].astype(jnp.bfloat16)


def stage_kernel(in_ref, out_ref, staged_in_ref, staged_out_ref):
    staged_in_ref[...] = in_ref[...]
    staged_out_ref[...] = out_ref[...]


def unit_order(me, chips):
    chip, core = lax.div(me, 2), lax.rem(me, 2)
    sign, twin = 1 - 2 * core, 1 - core
    opposite = 2 * lax.rem(chip + 4, chips)
    order = []
    for distance in (1, 2, 3):
        at = 2 * lax.rem(chip - sign * distance + chips, chips)
        order += [at + core, at + twin]
    order += [2 * chip + core, 2 * chip + twin, opposite + core]
    for distance in (1, 2, 3):
        at = 2 * lax.rem(chip + sign * distance + chips, chips)
        order += [at + twin, at + core]
    return order + [opposite + twin]


def sums_kernel(capacity, me_ref, got_ref, twin_got_ref, in_ref, twin_in_ref, out_ref, twin_out_ref,
                rows_ref, back_ref, own_ref, far_ref, near_ref, middle_ref, third_ref,
                twin_rows, twin_back):
    experts, _, width = got_ref.shape
    units = rows_ref.shape[0] // UNIT
    blocks = UNIT // capacity
    for k, unit in enumerate(unit_order(me_ref[0], units // 2)):
        here = slice(k * UNIT, (k + 1) * UNIT)
        for source, row_to, back_to in (
            (got_ref, rows_ref, back_ref),
            (twin_got_ref, twin_rows, twin_back),
        ):
            block = source[pl.ds(unit * blocks, blocks)].astype(jnp.float32)
            row_to[here, :] = block[:, :capacity].reshape(UNIT, width).astype(jnp.bfloat16)
            back_to[here, :] = block[:, capacity:].reshape(UNIT, width).astype(jnp.bfloat16)
    part = slice(6 * UNIT, 15 * UNIT)
    ff = out_ref.shape[0]

    def put(columns, total):
        own_ref[:, columns] = total[: 2 * UNIT]
        far_ref[:, columns] = total[2 * UNIT : 3 * UNIT].astype(jnp.bfloat16)
        near_ref[:, columns] = total[3 * UNIT : 5 * UNIT].astype(jnp.bfloat16)
        middle_ref[:, columns] = total[5 * UNIT : 7 * UNIT]
        third_ref[:, columns] = total[7 * UNIT :].astype(jnp.bfloat16)

    step = ff // 2
    for start in range(0, 2 * ff, step):
        columns = slice(start, start + step)
        put(
            columns,
            dot(rows_ref[part, :], in_ref[:, columns]) + dot(twin_rows[part, :], twin_in_ref[:, columns]),
        )
    for start in range(0, ff, step):
        some = slice(start, start + step)
        put(
            slice(2 * ff + start, 2 * ff + start + step),
            dot(back_ref[part, :], out_ref[some, :], LAST)
            + dot(twin_back[part, :], twin_out_ref[some, :], LAST),
        )


def gateway_kernel(middle_ref, third_ref, far_ref, sum_ref):
    total = middle_ref[...] + third_ref[...].astype(jnp.float32)
    sum_ref[:UNIT, :] = total[:UNIT].astype(jnp.bfloat16)
    sum_ref[UNIT:, :] = (total[UNIT:] + far_ref[...].astype(jnp.float32)).astype(jnp.bfloat16)


def arrived_kernel(near_ref, passed_ref, sum_ref):
    sum_ref[...] = near_ref[...].astype(jnp.float32) + passed_ref[...].astype(jnp.float32)


def swish_kernel(own_ref, arrived_ref, twin_ref, mid_ref):
    arrived, twin = arrived_ref[...], twin_ref[...]
    share = own_ref[...] + jnp.concatenate(
        [arrived[UNIT:] + twin[:UNIT], arrived[:UNIT] + twin[UNIT:]], axis=0
    )
    ff = share.shape[1] // 3
    gate_part, up_part, back_hidden = share[:, :ff], share[:, ff : 2 * ff], share[:, 2 * ff :]
    sigma = jax.nn.sigmoid(gate_part)
    activated = gate_part * sigma
    slope = sigma + gate_part * sigma * (1.0 - sigma)
    mid_ref[:, :ff] = (activated * up_part).astype(jnp.bfloat16)
    mid_ref[:, ff : 2 * ff] = (back_hidden * up_part * slope).astype(jnp.bfloat16)
    mid_ref[:, 2 * ff :] = (back_hidden * activated).astype(jnp.bfloat16)


def results_kernel(capacity, me_ref, in_ref, out_ref, *refs):
    parts, (back_ref, full_ref) = refs[:-2], refs[-2:]
    at = 0
    for part in parts:
        count = part.shape[0]
        full_ref[at : at + count, :] = part[...]
        at += count
    ff, width = out_ref.shape
    out = dot(full_ref[:, :ff], out_ref[...])
    grad = dot(full_ref[:, ff:], in_ref[...], LAST)
    units = full_ref.shape[0] // UNIT
    blocks = UNIT // capacity
    for k, unit in enumerate(unit_order(me_ref[0], units // 2)):
        here = slice(k * UNIT, (k + 1) * UNIT)
        back_ref[pl.ds(unit * blocks, blocks)] = jnp.concatenate(
            [
                out[here].reshape(blocks, capacity, width),
                grad[here].reshape(blocks, capacity, width),
            ],
            axis=1,
        ).astype(jnp.bfloat16)


def call(kernel, out_shape, flops, *operands, scratch=(), scalar_first=False, in_place=False):
    def size(a):
        return a.size * a.dtype.itemsize

    moved = sum(map(size, operands)) + sum(map(size, jax.tree.leaves(out_shape)))
    space = pl.ANY if in_place else pltpu.VMEM
    specs = [pl.BlockSpec(memory_space=space) for _ in operands]
    if scalar_first:
        specs[0] = pl.BlockSpec(memory_space=pltpu.SMEM)
    return pl.pallas_call(
        kernel,
        out_shape=out_shape,
        in_specs=specs,
        scratch_shapes=scratch,
        compiler_params=pltpu.CompilerParams(vmem_limit_bytes=(60 if in_place else 24) * 2**20),
        cost_estimate=pl.CostEstimate(flops=flops, bytes_accessed=moved, transcendentals=0),
    )(*operands)


def local(tokens, input_weight, output_weight, routes, gates, cotangent):
    block_tok, width = tokens.shape
    route_count = routes.shape[1]
    experts = lax.axis_size("fsdp")
    chips = lax.axis_size("expert") // 2
    ff = output_weight.shape[1]
    capacity = min(block_tok, 2 * block_tok * route_count // experts)
    rows = experts * capacity
    weight_in = input_weight[0]
    weight_out = output_weight[0]
    me = lax.axis_index("expert").reshape(1)
    bf16, f32 = jnp.bfloat16, jnp.float32

    def exchange(values):
        return lax.all_to_all(values, "fsdp", split_axis=0, concat_axis=0, tiled=True)

    def swap(values):
        return lax.ppermute(values, "expert", [(d, d ^ 1) for d in range(2 * chips)])

    def along(values, distance):
        up = [(2 * i, 2 * ((i + distance) % chips)) for i in range(chips)]
        down = [(2 * i + 1, 2 * ((i - distance) % chips) + 1) for i in range(chips)]
        return lax.ppermute(values, "expert", up + down)

    def array(count, columns, dtype):
        return jax.ShapeDtypeStruct((count, columns), dtype)

    sent, maps = call(
        lambda *refs: dispatch_kernel(capacity, *refs),
        (
            jax.ShapeDtypeStruct((experts, 2 * capacity, width), jnp.bfloat16),
            jax.ShapeDtypeStruct((rows, 4 * block_tok), jnp.bfloat16),
        ),
        10 * rows * block_tok * width,
        routes.T,
        gates.T,
        tokens,
        cotangent,
        scratch=[
            pltpu.VMEM((route_count, block_tok), jnp.int32),
            pltpu.VMEM((route_count, block_tok), f32),
            pltpu.VMEM((4 * block_tok, width), bf16),
            pltpu.VMEM((4 * block_tok, width), bf16),
            pltpu.SemaphoreType.DMA((4,)),
        ],
        in_place=True,
    )
    sent, *ready = lax.optimization_barrier((sent, weight_in, weight_out))
    staged = call(
        stage_kernel, (array(width, 2 * ff, bf16), array(ff, width, bf16)), width * ff, *ready
    )
    got, twin_in, twin_out = lax.optimization_barrier((exchange(sent), *map(swap, staged)))
    all_columns = 3 * ff
    routed_rows, routed_back, own, far, near, middle, third = call(
        lambda *refs: sums_kernel(capacity, *refs),
        (
            array(rows, width, bf16),
            array(rows, width, bf16),
            array(2 * UNIT, all_columns, f32),
            array(UNIT, all_columns, bf16),
            array(2 * UNIT, all_columns, bf16),
            array(2 * UNIT, all_columns, f32),
            array(2 * UNIT, all_columns, bf16),
        ),
        4 * 9 * UNIT * width * all_columns,
        me,
        got,
        swap(got),
        weight_in,
        twin_in,
        weight_out,
        twin_out,
        scratch=[pltpu.VMEM((rows, width), bf16), pltpu.VMEM((rows, width), bf16)],
        scalar_first=True,
    )
    third = along(third, 1)
    far = along(far, 2)
    near = along(near, 1)
    passed = along(
        call(gateway_kernel, array(2 * UNIT, all_columns, bf16), rows * ff, middle, third, far), 2
    )
    arrived = call(arrived_kernel, array(2 * UNIT, all_columns, f32), rows * ff, near, passed)
    chip_mid = call(
        swish_kernel, array(2 * UNIT, all_columns, bf16), rows * ff, own, arrived, swap(arrived)
    )

    second = along(chip_mid, 2)
    first = along(chip_mid, 1)
    third = along(second, 1)
    far = along(second[:UNIT], 2)
    back, full = call(
        lambda *refs: results_kernel(capacity, *refs),
        (
            jax.ShapeDtypeStruct((experts, 2 * capacity, width), bf16),
            array(rows, all_columns, bf16),
        ),
        2 * rows * width * all_columns,
        me,
        weight_in,
        weight_out,
        first,
        second,
        third,
        chip_mid,
        far,
        swap(first),
        swap(second),
        swap(third),
        swap(far),
        scalar_first=True,
    )
    home = exchange(back)
    hidden, grad_pre = full[:, :ff], full[:, ff:]
    grad_input = dot(routed_rows, grad_pre, FIRST).astype(bf16)[None]
    grad_output = dot(hidden, routed_back, FIRST).astype(bf16)[None]
    mixed, grad_tokens = call(
        lambda *refs: combine_kernel(capacity, *refs),
        (
            jax.ShapeDtypeStruct((block_tok, width), jnp.bfloat16),
            jax.ShapeDtypeStruct((block_tok, width), jnp.bfloat16),
        ),
        8 * rows * block_tok * width,
        maps,
        home,
    )
    return (mixed, grad_tokens, grad_input, grad_output)


def solution(mesh):
    placed = (
        P("fsdp", "expert"),
        P("fsdp", "expert", None),
        P("fsdp", None, "expert"),
        P("fsdp", None),
        P("fsdp", None),
        P("fsdp", "expert"),
    )
    return jax.shard_map(
        local,
        mesh=mesh,
        in_specs=placed,
        out_specs=(
            P("fsdp", "expert"),
            P("fsdp", "expert"),
            P("fsdp", "expert", None),
            P("fsdp", None, "expert"),
        ),
        check_vma=False,
    )
```

```python
import jax
import jax.numpy as jnp
from jax import lax
from jax.experimental import pallas as pl
from jax.experimental.pallas import tpu as pltpu
from jax.sharding import PartitionSpec as P

PLAIN = (((1,), (0,)), ((), ()))
LAST = (((1,), (1,)), ((), ()))
FIRST = (((0,), (0,)), ((), ()))
UNIT = 32


def dot(a, b, dims=PLAIN):
    return lax.dot_general(a, b, dims, preferred_element_type=jnp.float32)


def bf16_parts(values):
    first = values.astype(jnp.bfloat16)
    rest = values - first.astype(jnp.float32)
    second = rest.astype(jnp.bfloat16)
    third = (rest - second.astype(jnp.float32)).astype(jnp.bfloat16)
    return first, second, third


def dispatch_kernel(capacity, routes_hbm, gates_hbm, tokens_hbm, cotangent_hbm, sent_ref, maps_ref,
                    routes_ref, gates_ref, tokens_ref, cotangent_ref, arrived):
    experts, _, width = sent_ref.shape
    rows, lanes = maps_ref.shape
    route_count, count = routes_hbm.shape
    copies = [
        pltpu.make_async_copy(source, target, arrived.at[i])
        for i, (source, target) in enumerate(
            (
                (routes_hbm, routes_ref),
                (gates_hbm, gates_ref),
                (tokens_hbm, tokens_ref.at[3 * count : 4 * count]),
                (cotangent_hbm, cotangent_ref.at[3 * count : 4 * count]),
            )
        )
    ]
    for copy in copies:
        copy.start()
    tokens_ref[: 3 * count, :] = jnp.zeros((3 * count, width), jnp.bfloat16)
    cotangent_ref[: 3 * count, :] = jnp.zeros((3 * count, width), jnp.bfloat16)
    token = lax.broadcasted_iota(jnp.int32, (count, lanes), 0)
    lane = lax.broadcasted_iota(jnp.int32, (count, lanes), 1)
    group = [lane == token + i * count for i in range(4)]
    group = [jnp.where(one, 1.0, 0.0).astype(jnp.bfloat16) for one in group]
    first_row = lax.broadcasted_iota(jnp.int32, (rows, experts), 1) * capacity
    at = lax.broadcasted_iota(jnp.int32, (rows, experts), 0)
    inside = (at >= first_row) & (at < first_row + capacity)
    spread = jnp.where(inside, 1.0, 0.0).astype(jnp.bfloat16)
    local_slot = jnp.sum(jnp.where(inside, at - first_row, 0), axis=1, keepdims=True)
    copies[0].wait()
    copies[1].wait()
    everywhere = group[0] + group[1] + group[2] + group[3]
    routes = dot(routes_ref[...].astype(jnp.float32).astype(jnp.bfloat16), everywhere)
    ones = jnp.ones((route_count, count), jnp.bfloat16)
    values = jnp.zeros((route_count, lanes), jnp.float32)
    for part, lanes_of in zip((*bf16_parts(gates_ref[...]), ones), group):
        values = values + dot(part, lanes_of)
    expert = lax.broadcasted_iota(jnp.int32, (experts, lanes), 0).astype(jnp.float32)
    named = jnp.zeros((experts, lanes), jnp.float32)
    value_of = jnp.zeros((experts, lanes), jnp.float32)
    for k in range(route_count):
        hit = routes[k : k + 1, :] == expert
        named = jnp.where(hit, 1.0, named)
        value_of = jnp.where(hit, values[k : k + 1, :], value_of)
    other = lax.broadcasted_iota(jnp.int32, (lanes, lanes), 0)
    mine = lax.broadcasted_iota(jnp.int32, (lanes, lanes), 1)
    for _ in range(3):
        mine = jnp.where(mine >= count, mine - count, mine)
    before = jnp.where(other < mine, 1.0, 0.0).astype(jnp.bfloat16)
    named = named.astype(jnp.bfloat16)
    slot = dot(named, before).astype(jnp.bfloat16)
    picked = (dot(spread, named) > 0.5) & (dot(spread, slot) == local_slot.astype(jnp.float32))
    maps = jnp.where(picked, dot(spread, value_of.astype(jnp.bfloat16)), 0.0)
    is_gate = lax.broadcasted_iota(jnp.int32, (rows, lanes), 1) < 3 * count
    row_gate = jnp.sum(jnp.where(is_gate, maps, 0.0), axis=1, keepdims=True)
    maps = maps.astype(jnp.bfloat16)
    maps_ref[...] = maps
    copies[2].wait()
    copies[3].wait()
    send_rows = dot(maps, tokens_ref[...])
    send_back = row_gate * dot(maps, cotangent_ref[...])
    sent_ref[...] = jnp.concatenate(
        [send_rows.reshape(experts, capacity, width), send_back.reshape(experts, capacity, width)],
        axis=1,
    ).astype(jnp.bfloat16)


def combine_kernel(capacity, maps_ref, home_ref, mixed_ref, grad_ref):
    experts, _, width = home_ref.shape
    count = mixed_ref.shape[0]
    rows = experts * capacity
    home = home_ref[...].astype(jnp.float32)
    out = home[:, :capacity, :].reshape(rows, width).astype(jnp.bfloat16)
    grad = home[:, capacity:, :].reshape(rows, width).astype(jnp.bfloat16)
    total = dot(maps_ref[...], out, FIRST)
    total = total[:count] + total[count : 2 * count] + total[2 * count : 3 * count]
    mixed_ref[...] = total.astype(jnp.bfloat16)
    grad_ref[...] = dot(maps_ref[...], grad, FIRST)[3 * count :].astype(jnp.bfloat16)


def stage_kernel(in_ref, out_ref, staged_in_ref, staged_out_ref):
    staged_in_ref[...] = in_ref[...]
    staged_out_ref[...] = out_ref[...]


def unit_order(me, chips):
    chip, core = lax.div(me, 2), lax.rem(me, 2)
    sign, twin = 1 - 2 * core, 1 - core
    opposite = 2 * lax.rem(chip + 4, chips)
    order = []
    for distance in (1, 2, 3):
        at = 2 * lax.rem(chip - sign * distance + chips, chips)
        order += [at + core, at + twin]
    order += [2 * chip + core, 2 * chip + twin, opposite + core]
    for distance in (1, 2, 3):
        at = 2 * lax.rem(chip + sign * distance + chips, chips)
        order += [at + twin, at + core]
    return order + [opposite + twin]


def sums_kernel(capacity, me_ref, got_ref, twin_got_ref, in_ref, twin_in_ref, out_ref, twin_out_ref,
                rows_ref, back_ref, own_ref, far_ref, near_ref, middle_ref, third_ref,
                twin_rows, twin_back):
    experts, _, width = got_ref.shape
    units = rows_ref.shape[0] // UNIT
    blocks = UNIT // capacity
    for k, unit in enumerate(unit_order(me_ref[0], units // 2)):
        here = slice(k * UNIT, (k + 1) * UNIT)
        for source, row_to, back_to in (
            (got_ref, rows_ref, back_ref),
            (twin_got_ref, twin_rows, twin_back),
        ):
            block = source[pl.ds(unit * blocks, blocks)].astype(jnp.float32)
            row_to[here, :] = block[:, :capacity].reshape(UNIT, width).astype(jnp.bfloat16)
            back_to[here, :] = block[:, capacity:].reshape(UNIT, width).astype(jnp.bfloat16)
    part = slice(6 * UNIT, 15 * UNIT)
    ff = out_ref.shape[0]

    def put(columns, total):
        own_ref[:, columns] = total[: 2 * UNIT]
        far_ref[:, columns] = total[2 * UNIT : 3 * UNIT].astype(jnp.bfloat16)
        near_ref[:, columns] = total[3 * UNIT : 5 * UNIT].astype(jnp.bfloat16)
        middle_ref[:, columns] = total[5 * UNIT : 7 * UNIT]
        third_ref[:, columns] = total[7 * UNIT :].astype(jnp.bfloat16)

    step = ff // 2
    for start in range(0, 2 * ff, step):
        columns = slice(start, start + step)
        put(
            columns,
            dot(rows_ref[part, :], in_ref[:, columns]) + dot(twin_rows[part, :], twin_in_ref[:, columns]),
        )
    for start in range(0, ff, step):
        some = slice(start, start + step)
        put(
            slice(2 * ff + start, 2 * ff + start + step),
            dot(back_ref[part, :], out_ref[some, :], LAST)
            + dot(twin_back[part, :], twin_out_ref[some, :], LAST),
        )


def gateway_kernel(middle_ref, third_ref, far_ref, sum_ref):
    total = middle_ref[...] + third_ref[...].astype(jnp.float32)
    sum_ref[:UNIT, :] = total[:UNIT].astype(jnp.bfloat16)
    sum_ref[UNIT:, :] = (total[UNIT:] + far_ref[...].astype(jnp.float32)).astype(jnp.bfloat16)


def arrived_kernel(near_ref, passed_ref, sum_ref):
    sum_ref[...] = near_ref[...].astype(jnp.float32) + passed_ref[...].astype(jnp.float32)


def swish_kernel(own_ref, arrived_ref, twin_ref, mid_ref):
    arrived, twin = arrived_ref[...], twin_ref[...]
    share = own_ref[...] + jnp.concatenate(
        [arrived[UNIT:] + twin[:UNIT], arrived[:UNIT] + twin[UNIT:]], axis=0
    )
    ff = share.shape[1] // 3
    gate_part, up_part, back_hidden = share[:, :ff], share[:, ff : 2 * ff], share[:, 2 * ff :]
    sigma = jax.nn.sigmoid(gate_part)
    activated = gate_part * sigma
    slope = sigma + gate_part * sigma * (1.0 - sigma)
    mid_ref[:, :ff] = (activated * up_part).astype(jnp.bfloat16)
    mid_ref[:, ff : 2 * ff] = (back_hidden * up_part * slope).astype(jnp.bfloat16)
    mid_ref[:, 2 * ff :] = (back_hidden * activated).astype(jnp.bfloat16)


def results_kernel(capacity, me_ref, in_ref, out_ref, *refs):
    parts, (back_ref, full_ref) = refs[:-2], refs[-2:]
    at = 0
    for part in parts:
        count = part.shape[0]
        full_ref[at : at + count, :] = part[...]
        at += count
    ff, width = out_ref.shape
    out = dot(full_ref[:, :ff], out_ref[...])
    grad = dot(full_ref[:, ff:], in_ref[...], LAST)
    units = full_ref.shape[0] // UNIT
    blocks = UNIT // capacity
    for k, unit in enumerate(unit_order(me_ref[0], units // 2)):
        here = slice(k * UNIT, (k + 1) * UNIT)
        back_ref[pl.ds(unit * blocks, blocks)] = jnp.concatenate(
            [
                out[here].reshape(blocks, capacity, width),
                grad[here].reshape(blocks, capacity, width),
            ],
            axis=1,
        ).astype(jnp.bfloat16)


def call(kernel, out_shape, flops, *operands, scratch=(), scalar_first=False, in_place=False):
    def size(a):
        return a.size * a.dtype.itemsize

    moved = sum(map(size, operands)) + sum(map(size, jax.tree.leaves(out_shape)))
    space = pl.ANY if in_place else pltpu.VMEM
    specs = [pl.BlockSpec(memory_space=space) for _ in operands]
    if scalar_first:
        specs[0] = pl.BlockSpec(memory_space=pltpu.SMEM)
    return pl.pallas_call(
        kernel,
        out_shape=out_shape,
        in_specs=specs,
        scratch_shapes=scratch,
        compiler_params=pltpu.CompilerParams(vmem_limit_bytes=(60 if in_place else 24) * 2**20),
        cost_estimate=pl.CostEstimate(flops=flops, bytes_accessed=moved, transcendentals=0),
    )(*operands)


def local(tokens, input_weight, output_weight, routes, gates, cotangent):
    block_tok, width = tokens.shape
    route_count = routes.shape[1]
    experts = lax.axis_size("fsdp")
    chips = lax.axis_size("expert") // 2
    ff = output_weight.shape[1]
    capacity = min(block_tok, 2 * block_tok * route_count // experts)
    rows = experts * capacity
    weight_in = input_weight[0]
    weight_out = output_weight[0]
    me = lax.axis_index("expert").reshape(1)
    bf16, f32 = jnp.bfloat16, jnp.float32

    def exchange(values):
        return lax.all_to_all(values, "fsdp", split_axis=0, concat_axis=0, tiled=True)

    def swap(values):
        return lax.ppermute(values, "expert", [(d, d ^ 1) for d in range(2 * chips)])

    def along(values, distance):
        up = [(2 * i, 2 * ((i + distance) % chips)) for i in range(chips)]
        down = [(2 * i + 1, 2 * ((i - distance) % chips) + 1) for i in range(chips)]
        return lax.ppermute(values, "expert", up + down)

    def array(count, columns, dtype):
        return jax.ShapeDtypeStruct((count, columns), dtype)

    sent, maps = call(
        lambda *refs: dispatch_kernel(capacity, *refs),
        (
            jax.ShapeDtypeStruct((experts, 2 * capacity, width), jnp.bfloat16),
            jax.ShapeDtypeStruct((rows, 4 * block_tok), jnp.bfloat16),
        ),
        10 * rows * block_tok * width,
        routes.T,
        gates.T,
        tokens,
        cotangent,
        scratch=[
            pltpu.VMEM((route_count, block_tok), jnp.int32),
            pltpu.VMEM((route_count, block_tok), f32),
            pltpu.VMEM((4 * block_tok, width), bf16),
            pltpu.VMEM((4 * block_tok, width), bf16),
            pltpu.SemaphoreType.DMA((4,)),
        ],
        in_place=True,
    )
    sent, *ready = lax.optimization_barrier((sent, weight_in, weight_out))
    staged = call(
        stage_kernel, (array(width, 2 * ff, bf16), array(ff, width, bf16)), width * ff, *ready
    )
    got, twin_in, twin_out = lax.optimization_barrier((exchange(sent), *map(swap, staged)))
    all_columns = 3 * ff
    routed_rows, routed_back, own, far, near, middle, third = call(
        lambda *refs: sums_kernel(capacity, *refs),
        (
            array(rows, width, bf16),
            array(rows, width, bf16),
            array(2 * UNIT, all_columns, f32),
            array(UNIT, all_columns, bf16),
            array(2 * UNIT, all_columns, bf16),
            array(2 * UNIT, all_columns, f32),
            array(2 * UNIT, all_columns, bf16),
        ),
        4 * 9 * UNIT * width * all_columns,
        me,
        got,
        swap(got),
        weight_in,
        twin_in,
        weight_out,
        twin_out,
        scratch=[pltpu.VMEM((rows, width), bf16), pltpu.VMEM((rows, width), bf16)],
        scalar_first=True,
    )
    third = along(third, 1)
    far = along(far, 2)
    near = along(near, 1)
    passed = along(
        call(gateway_kernel, array(2 * UNIT, all_columns, bf16), rows * ff, middle, third, far), 2
    )
    arrived = call(arrived_kernel, array(2 * UNIT, all_columns, f32), rows * ff, near, passed)
    chip_mid = call(
        swish_kernel, array(2 * UNIT, all_columns, bf16), rows * ff, own, arrived, swap(arrived)
    )

    first = along(chip_mid, 1)
    second = along(chip_mid, 2)
    third = along(first, 2)
    far = along(second[:UNIT], 2)
    back, full = call(
        lambda *refs: results_kernel(capacity, *refs),
        (
            jax.ShapeDtypeStruct((experts, 2 * capacity, width), bf16),
            array(rows, all_columns, bf16),
        ),
        2 * rows * width * all_columns,
        me,
        weight_in,
        weight_out,
        first,
        second,
        third,
        chip_mid,
        far,
        swap(first),
        swap(second),
        swap(third),
        swap(far),
        scalar_first=True,
    )
    home = exchange(back)
    hidden, grad_pre = full[:, :ff], full[:, ff:]
    grad_input = dot(routed_rows, grad_pre, FIRST).astype(bf16)[None]
    grad_output = dot(hidden, routed_back, FIRST).astype(bf16)[None]
    mixed, grad_tokens = call(
        lambda *refs: combine_kernel(capacity, *refs),
        (
            jax.ShapeDtypeStruct((block_tok, width), jnp.bfloat16),
            jax.ShapeDtypeStruct((block_tok, width), jnp.bfloat16),
        ),
        8 * rows * block_tok * width,
        maps,
        home,
    )
    return (mixed, grad_tokens, grad_input, grad_output)


def solution(mesh):
    placed = (
        P("fsdp", "expert"),
        P("fsdp", "expert", None),
        P("fsdp", None, "expert"),
        P("fsdp", None),
        P("fsdp", None),
        P("fsdp", "expert"),
    )
    return jax.shard_map(
        local,
        mesh=mesh,
        in_specs=placed,
        out_specs=(
            P("fsdp", "expert"),
            P("fsdp", "expert"),
            P("fsdp", "expert", None),
            P("fsdp", None, "expert"),
        ),
        check_vma=False,
    )
```

```python
import jax
import jax.numpy as jnp
from jax import lax
from jax.experimental import pallas as pl
from jax.experimental.pallas import tpu as pltpu
from jax.sharding import PartitionSpec as P

PLAIN = (((1,), (0,)), ((), ()))
LAST = (((1,), (1,)), ((), ()))
FIRST = (((0,), (0,)), ((), ()))
UNIT = 32


def dot(a, b, dims=PLAIN):
    return lax.dot_general(a, b, dims, preferred_element_type=jnp.float32)


def bf16_parts(values):
    first = values.astype(jnp.bfloat16)
    rest = values - first.astype(jnp.float32)
    second = rest.astype(jnp.bfloat16)
    third = (rest - second.astype(jnp.float32)).astype(jnp.bfloat16)
    return first, second, third


def dispatch_kernel(capacity, routes_hbm, gates_hbm, tokens_hbm, cotangent_hbm, sent_ref, maps_ref,
                    routes_ref, gates_ref, tokens_ref, cotangent_ref, arrived):
    experts, _, width = sent_ref.shape
    rows, lanes = maps_ref.shape
    route_count, count = routes_hbm.shape
    copies = [
        pltpu.make_async_copy(source, target, arrived.at[i])
        for i, (source, target) in enumerate(
            (
                (routes_hbm, routes_ref),
                (gates_hbm, gates_ref),
                (tokens_hbm, tokens_ref.at[3 * count : 4 * count]),
                (cotangent_hbm, cotangent_ref.at[3 * count : 4 * count]),
            )
        )
    ]
    for copy in copies:
        copy.start()
    tokens_ref[: 3 * count, :] = jnp.zeros((3 * count, width), jnp.bfloat16)
    cotangent_ref[: 3 * count, :] = jnp.zeros((3 * count, width), jnp.bfloat16)
    token = lax.broadcasted_iota(jnp.int32, (count, lanes), 0)
    lane = lax.broadcasted_iota(jnp.int32, (count, lanes), 1)
    group = [lane == token + i * count for i in range(4)]
    group = [jnp.where(one, 1.0, 0.0).astype(jnp.bfloat16) for one in group]
    first_row = lax.broadcasted_iota(jnp.int32, (rows, experts), 1) * capacity
    at = lax.broadcasted_iota(jnp.int32, (rows, experts), 0)
    inside = (at >= first_row) & (at < first_row + capacity)
    spread = jnp.where(inside, 1.0, 0.0).astype(jnp.bfloat16)
    local_slot = jnp.sum(jnp.where(inside, at - first_row, 0), axis=1, keepdims=True)
    copies[0].wait()
    copies[1].wait()
    everywhere = group[0] + group[1] + group[2] + group[3]
    routes = dot(routes_ref[...].astype(jnp.float32).astype(jnp.bfloat16), everywhere)
    ones = jnp.ones((route_count, count), jnp.bfloat16)
    values = jnp.zeros((route_count, lanes), jnp.float32)
    for part, lanes_of in zip((*bf16_parts(gates_ref[...]), ones), group):
        values = values + dot(part, lanes_of)
    expert = lax.broadcasted_iota(jnp.int32, (experts, lanes), 0).astype(jnp.float32)
    named = jnp.zeros((experts, lanes), jnp.float32)
    value_of = jnp.zeros((experts, lanes), jnp.float32)
    for k in range(route_count):
        hit = routes[k : k + 1, :] == expert
        named = jnp.where(hit, 1.0, named)
        value_of = jnp.where(hit, values[k : k + 1, :], value_of)
    other = lax.broadcasted_iota(jnp.int32, (lanes, lanes), 0)
    mine = lax.broadcasted_iota(jnp.int32, (lanes, lanes), 1)
    for _ in range(3):
        mine = jnp.where(mine >= count, mine - count, mine)
    before = jnp.where(other < mine, 1.0, 0.0).astype(jnp.bfloat16)
    named = named.astype(jnp.bfloat16)
    slot = dot(named, before).astype(jnp.bfloat16)
    picked = (dot(spread, named) > 0.5) & (dot(spread, slot) == local_slot.astype(jnp.float32))
    maps = jnp.where(picked, dot(spread, value_of.astype(jnp.bfloat16)), 0.0)
    is_gate = lax.broadcasted_iota(jnp.int32, (rows, lanes), 1) < 3 * count
    row_gate = jnp.sum(jnp.where(is_gate, maps, 0.0), axis=1, keepdims=True)
    maps = maps.astype(jnp.bfloat16)
    maps_ref[...] = maps
    copies[2].wait()
    copies[3].wait()
    send_rows = dot(maps, tokens_ref[...])
    send_back = row_gate * dot(maps, cotangent_ref[...])
    sent_ref[...] = jnp.concatenate(
        [send_rows.reshape(experts, capacity, width), send_back.reshape(experts, capacity, width)],
        axis=1,
    ).astype(jnp.bfloat16)


def combine_kernel(capacity, maps_ref, home_ref, mixed_ref, grad_ref):
    experts, _, width = home_ref.shape
    count = mixed_ref.shape[0]
    rows = experts * capacity
    home = home_ref[...].astype(jnp.float32)
    out = home[:, :capacity, :].reshape(rows, width).astype(jnp.bfloat16)
    grad = home[:, capacity:, :].reshape(rows, width).astype(jnp.bfloat16)
    total = dot(maps_ref[...], out, FIRST)
    total = total[:count] + total[count : 2 * count] + total[2 * count : 3 * count]
    mixed_ref[...] = total.astype(jnp.bfloat16)
    grad_ref[...] = dot(maps_ref[...], grad, FIRST)[3 * count :].astype(jnp.bfloat16)


def stage_kernel(in_ref, out_ref, staged_in_ref, staged_out_ref):
    staged_in_ref[...] = in_ref[...]
    staged_out_ref[...] = out_ref[...]


def unit_order(me, chips):
    chip, core = lax.div(me, 2), lax.rem(me, 2)
    sign, twin = 1 - 2 * core, 1 - core
    opposite = 2 * lax.rem(chip + 4, chips)
    order = []
    for distance in (1, 2, 3):
        at = 2 * lax.rem(chip - sign * distance + chips, chips)
        order += [at + core, at + twin]
    order += [2 * chip + core, 2 * chip + twin, opposite + core]
    for distance in (1, 2, 3):
        at = 2 * lax.rem(chip + sign * distance + chips, chips)
        order += [at + twin, at + core]
    return order + [opposite + twin]


def sums_kernel(capacity, me_ref, got_ref, twin_got_ref, in_ref, twin_in_ref, out_ref, twin_out_ref,
                own_ref, far_ref, near_ref, middle_ref, third_ref, rows_ref, back_ref, twin_rows,
                twin_back):
    experts, _, width = got_ref.shape
    units = experts * capacity // UNIT
    blocks = UNIT // capacity
    for k, unit in enumerate(unit_order(me_ref[0], units // 2)[6:15]):
        here = slice(k * UNIT, (k + 1) * UNIT)
        for source, row_to, back_to in (
            (got_ref, rows_ref, back_ref),
            (twin_got_ref, twin_rows, twin_back),
        ):
            block = source[pl.ds(unit * blocks, blocks)].astype(jnp.float32)
            row_to[here, :] = block[:, :capacity].reshape(UNIT, width).astype(jnp.bfloat16)
            back_to[here, :] = block[:, capacity:].reshape(UNIT, width).astype(jnp.bfloat16)
    ff = out_ref.shape[0]

    def put(columns, total):
        own_ref[:, columns] = total[: 2 * UNIT]
        far_ref[:, columns] = total[2 * UNIT : 3 * UNIT].astype(jnp.bfloat16)
        near_ref[:, columns] = total[3 * UNIT : 5 * UNIT].astype(jnp.bfloat16)
        middle_ref[:, columns] = total[5 * UNIT : 7 * UNIT]
        third_ref[:, columns] = total[7 * UNIT :].astype(jnp.bfloat16)

    step = ff // 2
    for start in range(0, 2 * ff, step):
        columns = slice(start, start + step)
        put(
            columns,
            dot(rows_ref[...], in_ref[:, columns]) + dot(twin_rows[...], twin_in_ref[:, columns]),
        )
    for start in range(0, ff, step):
        some = slice(start, start + step)
        put(
            slice(2 * ff + start, 2 * ff + start + step),
            dot(back_ref[...], out_ref[some, :], LAST)
            + dot(twin_back[...], twin_out_ref[some, :], LAST),
        )


def gateway_kernel(middle_ref, third_ref, far_ref, sum_ref):
    total = middle_ref[...] + third_ref[...].astype(jnp.float32)
    sum_ref[:UNIT, :] = total[:UNIT].astype(jnp.bfloat16)
    sum_ref[UNIT:, :] = (total[UNIT:] + far_ref[...].astype(jnp.float32)).astype(jnp.bfloat16)


def arrived_kernel(near_ref, passed_ref, sum_ref):
    sum_ref[...] = near_ref[...].astype(jnp.float32) + passed_ref[...].astype(jnp.float32)


def swish_kernel(own_ref, arrived_ref, twin_ref, mid_ref):
    arrived, twin = arrived_ref[...], twin_ref[...]
    share = own_ref[...] + jnp.concatenate(
        [arrived[UNIT:] + twin[:UNIT], arrived[:UNIT] + twin[UNIT:]], axis=0
    )
    ff = share.shape[1] // 3
    gate_part, up_part, back_hidden = share[:, :ff], share[:, ff : 2 * ff], share[:, 2 * ff :]
    sigma = jax.nn.sigmoid(gate_part)
    activated = gate_part * sigma
    slope = sigma + gate_part * sigma * (1.0 - sigma)
    mid_ref[:, :ff] = (activated * up_part).astype(jnp.bfloat16)
    mid_ref[:, ff : 2 * ff] = (back_hidden * up_part * slope).astype(jnp.bfloat16)
    mid_ref[:, 2 * ff :] = (back_hidden * activated).astype(jnp.bfloat16)


def results_kernel(capacity, me_ref, in_ref, out_ref, *refs):
    parts, (back_ref, full_out, full_ref, stored) = refs[:-4], refs[-4:]
    rows = full_ref.shape[0]
    order = iter(unit_order(me_ref[0], rows // (2 * UNIT)))
    for part in parts:
        for at in range(0, part.shape[0], UNIT):
            to = pl.multiple_of(next(order) * UNIT, UNIT)
            full_ref[pl.ds(to, UNIT), :] = part[at : at + UNIT, :]
    ff, width = out_ref.shape
    copy = pltpu.make_async_copy(full_ref, full_out, stored)
    copy.start()
    out = dot(full_ref[:, :ff], out_ref[...])
    grad = dot(full_ref[:, ff:], in_ref[...], LAST)
    experts = rows // capacity
    back_ref[...] = jnp.concatenate(
        [out.reshape(experts, capacity, width), grad.reshape(experts, capacity, width)], axis=1
    ).astype(jnp.bfloat16)
    copy.wait()


def call(kernel, out_shape, flops, *operands, scratch=(), scalar_first=False, in_place=False,
         outside=()):
    def size(a):
        return a.size * a.dtype.itemsize

    moved = sum(map(size, operands)) + sum(map(size, jax.tree.leaves(out_shape)))
    space = pl.ANY if in_place else pltpu.VMEM
    specs = [pl.BlockSpec(memory_space=space) for _ in operands]
    if scalar_first:
        specs[0] = pl.BlockSpec(memory_space=pltpu.SMEM)
    out_specs = tuple(
        pl.BlockSpec(memory_space=pl.ANY if i in outside else pltpu.VMEM)
        for i in range(len(jax.tree.leaves(out_shape)))
    )
    return pl.pallas_call(
        kernel,
        out_shape=out_shape,
        in_specs=specs,
        out_specs=out_specs if isinstance(out_shape, tuple) else out_specs[0],
        scratch_shapes=scratch,
        compiler_params=pltpu.CompilerParams(vmem_limit_bytes=(60 if in_place else 48) * 2**20),
        cost_estimate=pl.CostEstimate(flops=flops, bytes_accessed=moved, transcendentals=0),
    )(*operands)


def local(tokens, input_weight, output_weight, routes, gates, cotangent):
    block_tok, width = tokens.shape
    route_count = routes.shape[1]
    experts = lax.axis_size("fsdp")
    chips = lax.axis_size("expert") // 2
    ff = output_weight.shape[1]
    capacity = min(block_tok, 2 * block_tok * route_count // experts)
    rows = experts * capacity
    weight_in = input_weight[0]
    weight_out = output_weight[0]
    me = lax.axis_index("expert").reshape(1)
    bf16, f32 = jnp.bfloat16, jnp.float32

    def exchange(values):
        return lax.all_to_all(values, "fsdp", split_axis=0, concat_axis=0, tiled=True)

    def swap(values):
        return lax.ppermute(values, "expert", [(d, d ^ 1) for d in range(2 * chips)])

    def along(values, distance):
        up = [(2 * i, 2 * ((i + distance) % chips)) for i in range(chips)]
        down = [(2 * i + 1, 2 * ((i - distance) % chips) + 1) for i in range(chips)]
        return lax.ppermute(values, "expert", up + down)

    def array(count, columns, dtype):
        return jax.ShapeDtypeStruct((count, columns), dtype)

    sent, maps = call(
        lambda *refs: dispatch_kernel(capacity, *refs),
        (
            jax.ShapeDtypeStruct((experts, 2 * capacity, width), jnp.bfloat16),
            jax.ShapeDtypeStruct((rows, 4 * block_tok), jnp.bfloat16),
        ),
        10 * rows * block_tok * width,
        routes.T,
        gates.T,
        tokens,
        cotangent,
        scratch=[
            pltpu.VMEM((route_count, block_tok), jnp.int32),
            pltpu.VMEM((route_count, block_tok), f32),
            pltpu.VMEM((4 * block_tok, width), bf16),
            pltpu.VMEM((4 * block_tok, width), bf16),
            pltpu.SemaphoreType.DMA((4,)),
        ],
        in_place=True,
    )
    sent, *ready = lax.optimization_barrier((sent, weight_in, weight_out))
    staged = call(
        stage_kernel, (array(width, 2 * ff, bf16), array(ff, width, bf16)), width * ff, *ready
    )
    got, twin_in, twin_out = lax.optimization_barrier((exchange(sent), *map(swap, staged)))
    all_columns = 3 * ff
    routed_rows = got[:, :capacity].reshape(rows, width)
    routed_back = got[:, capacity:].reshape(rows, width)
    own, far, near, middle, third = call(
        lambda *refs: sums_kernel(capacity, *refs),
        (
            array(2 * UNIT, all_columns, f32),
            array(UNIT, all_columns, bf16),
            array(2 * UNIT, all_columns, bf16),
            array(2 * UNIT, all_columns, f32),
            array(2 * UNIT, all_columns, bf16),
        ),
        4 * 9 * UNIT * width * all_columns,
        me,
        got,
        swap(got),
        weight_in,
        twin_in,
        weight_out,
        twin_out,
        scratch=[pltpu.VMEM((9 * UNIT, width), bf16)] * 4,
        scalar_first=True,
    )
    third = along(third, 1)
    far = along(far, 2)
    near = along(near, 1)
    passed = along(
        call(gateway_kernel, array(2 * UNIT, all_columns, bf16), rows * ff, middle, third, far), 2
    )
    arrived = call(arrived_kernel, array(2 * UNIT, all_columns, f32), rows * ff, near, passed)
    chip_mid = call(
        swish_kernel, array(2 * UNIT, all_columns, bf16), rows * ff, own, arrived, swap(arrived)
    )

    second = along(chip_mid, 2)
    first = along(chip_mid, 1)
    third = along(second, 1)
    far = along(second[:UNIT], 2)
    back, full = call(
        lambda *refs: results_kernel(capacity, *refs),
        (
            jax.ShapeDtypeStruct((experts, 2 * capacity, width), bf16),
            array(rows, all_columns, bf16),
        ),
        2 * rows * width * all_columns,
        me,
        weight_in,
        weight_out,
        first,
        second,
        third,
        chip_mid,
        far,
        swap(first),
        swap(second),
        swap(third),
        swap(far),
        scratch=[pltpu.VMEM((rows, all_columns), bf16), pltpu.SemaphoreType.DMA],
        scalar_first=True,
        outside=(1,),
    )
    home = exchange(back)
    hidden, grad_pre = full[:, :ff], full[:, ff:]
    grad_input = dot(routed_rows, grad_pre, FIRST).astype(bf16)[None]
    grad_output = dot(hidden, routed_back, FIRST).astype(bf16)[None]
    mixed, grad_tokens = call(
        lambda *refs: combine_kernel(capacity, *refs),
        (
            jax.ShapeDtypeStruct((block_tok, width), jnp.bfloat16),
            jax.ShapeDtypeStruct((block_tok, width), jnp.bfloat16),
        ),
        8 * rows * block_tok * width,
        maps,
        home,
    )
    return (mixed, grad_tokens, grad_input, grad_output)


def solution(mesh):
    placed = (
        P("fsdp", "expert"),
        P("fsdp", "expert", None),
        P("fsdp", None, "expert"),
        P("fsdp", None),
        P("fsdp", None),
        P("fsdp", "expert"),
    )
    return jax.shard_map(
        local,
        mesh=mesh,
        in_specs=placed,
        out_specs=(
            P("fsdp", "expert"),
            P("fsdp", "expert"),
            P("fsdp", "expert", None),
            P("fsdp", None, "expert"),
        ),
        check_vma=False,
    )
```

```python
import jax
import jax.numpy as jnp
from jax import lax
from jax.experimental import pallas as pl
from jax.experimental.pallas import tpu as pltpu
from jax.sharding import PartitionSpec as P

PLAIN = (((1,), (0,)), ((), ()))
LAST = (((1,), (1,)), ((), ()))
FIRST = (((0,), (0,)), ((), ()))
UNIT = 32


def dot(a, b, dims=PLAIN):
    return lax.dot_general(a, b, dims, preferred_element_type=jnp.float32)


def bf16_parts(values):
    first = values.astype(jnp.bfloat16)
    rest = values - first.astype(jnp.float32)
    second = rest.astype(jnp.bfloat16)
    third = (rest - second.astype(jnp.float32)).astype(jnp.bfloat16)
    return first, second, third


def dispatch_kernel(capacity, routes_hbm, gates_hbm, tokens_hbm, cotangent_hbm, sent_ref, maps_ref,
                    routes_ref, gates_ref, tokens_ref, cotangent_ref, arrived):
    experts, _, width = sent_ref.shape
    rows, lanes = maps_ref.shape
    route_count, count = routes_hbm.shape
    copies = [
        pltpu.make_async_copy(source, target, arrived.at[i])
        for i, (source, target) in enumerate(
            (
                (routes_hbm, routes_ref),
                (gates_hbm, gates_ref),
                (tokens_hbm, tokens_ref.at[3 * count : 4 * count]),
                (cotangent_hbm, cotangent_ref.at[3 * count : 4 * count]),
            )
        )
    ]
    for copy in copies:
        copy.start()
    tokens_ref[: 3 * count, :] = jnp.zeros((3 * count, width), jnp.bfloat16)
    cotangent_ref[: 3 * count, :] = jnp.zeros((3 * count, width), jnp.bfloat16)
    token = lax.broadcasted_iota(jnp.int32, (count, lanes), 0)
    lane = lax.broadcasted_iota(jnp.int32, (count, lanes), 1)
    group = [lane == token + i * count for i in range(4)]
    group = [jnp.where(one, 1.0, 0.0).astype(jnp.bfloat16) for one in group]
    first_row = lax.broadcasted_iota(jnp.int32, (rows, experts), 1) * capacity
    at = lax.broadcasted_iota(jnp.int32, (rows, experts), 0)
    inside = (at >= first_row) & (at < first_row + capacity)
    spread = jnp.where(inside, 1.0, 0.0).astype(jnp.bfloat16)
    local_slot = jnp.sum(jnp.where(inside, at - first_row, 0), axis=1, keepdims=True)
    copies[0].wait()
    copies[1].wait()
    everywhere = group[0] + group[1] + group[2] + group[3]
    routes = dot(routes_ref[...].astype(jnp.float32).astype(jnp.bfloat16), everywhere)
    ones = jnp.ones((route_count, count), jnp.bfloat16)
    values = jnp.zeros((route_count, lanes), jnp.float32)
    for part, lanes_of in zip((*bf16_parts(gates_ref[...]), ones), group):
        values = values + dot(part, lanes_of)
    expert = lax.broadcasted_iota(jnp.int32, (experts, lanes), 0).astype(jnp.float32)
    named = jnp.zeros((experts, lanes), jnp.float32)
    value_of = jnp.zeros((experts, lanes), jnp.float32)
    for k in range(route_count):
        hit = routes[k : k + 1, :] == expert
        named = jnp.where(hit, 1.0, named)
        value_of = jnp.where(hit, values[k : k + 1, :], value_of)
    other = lax.broadcasted_iota(jnp.int32, (lanes, lanes), 0)
    mine = lax.broadcasted_iota(jnp.int32, (lanes, lanes), 1)
    for _ in range(3):
        mine = jnp.where(mine >= count, mine - count, mine)
    before = jnp.where(other < mine, 1.0, 0.0).astype(jnp.bfloat16)
    named = named.astype(jnp.bfloat16)
    slot = dot(named, before).astype(jnp.bfloat16)
    picked = (dot(spread, named) > 0.5) & (dot(spread, slot) == local_slot.astype(jnp.float32))
    maps = jnp.where(picked, dot(spread, value_of.astype(jnp.bfloat16)), 0.0)
    is_gate = lax.broadcasted_iota(jnp.int32, (rows, lanes), 1) < 3 * count
    row_gate = jnp.sum(jnp.where(is_gate, maps, 0.0), axis=1, keepdims=True)
    maps = maps.astype(jnp.bfloat16)
    maps_ref[...] = maps
    copies[2].wait()
    copies[3].wait()
    send_rows = dot(maps, tokens_ref[...])
    send_back = row_gate * dot(maps, cotangent_ref[...])
    sent_ref[...] = jnp.concatenate(
        [send_rows.reshape(experts, capacity, width), send_back.reshape(experts, capacity, width)],
        axis=1,
    ).astype(jnp.bfloat16)


def combine_kernel(capacity, maps_ref, home_ref, mixed_ref, grad_ref):
    experts, _, width = home_ref.shape
    count = mixed_ref.shape[0]
    rows = experts * capacity
    home = home_ref[...].astype(jnp.float32)
    out = home[:, :capacity, :].reshape(rows, width).astype(jnp.bfloat16)
    grad = home[:, capacity:, :].reshape(rows, width).astype(jnp.bfloat16)
    total = dot(maps_ref[...], out, FIRST)
    total = total[:count] + total[count : 2 * count] + total[2 * count : 3 * count]
    mixed_ref[...] = total.astype(jnp.bfloat16)
    grad_ref[...] = dot(maps_ref[...], grad, FIRST)[3 * count :].astype(jnp.bfloat16)


def stage_kernel(in_ref, out_ref, staged_in_ref, staged_out_ref):
    staged_in_ref[...] = in_ref[...]
    staged_out_ref[...] = out_ref[...]


def unit_order(me, chips):
    chip, core = lax.div(me, 2), lax.rem(me, 2)
    sign, twin = 1 - 2 * core, 1 - core
    opposite = 2 * lax.rem(chip + 4, chips)
    order = []
    for distance in (1, 2, 3):
        at = 2 * lax.rem(chip - sign * distance + chips, chips)
        order += [at + core, at + twin]
    order += [2 * chip + core, 2 * chip + twin, opposite + core]
    for distance in (1, 2, 3):
        at = 2 * lax.rem(chip + sign * distance + chips, chips)
        order += [at + twin, at + core]
    return order + [opposite + twin]


def sums_kernel(capacity, me_ref, got_ref, twin_got_ref, in_ref, twin_in_ref, out_ref, twin_out_ref,
                both_ref, own_ref, far_ref, near_ref, middle_ref, third_ref, twin_ref):
    experts, _, width = got_ref.shape
    units = both_ref.shape[0] // UNIT
    blocks = UNIT // capacity
    for k, unit in enumerate(unit_order(me_ref[0], units // 2)):
        here = slice(k * UNIT, (k + 1) * UNIT)
        for source, target in ((got_ref, both_ref), (twin_got_ref, twin_ref)):
            block = source[pl.ds(unit * blocks, blocks)].astype(jnp.float32)
            target[here, :width] = block[:, :capacity].reshape(UNIT, width).astype(jnp.bfloat16)
            target[here, width:] = block[:, capacity:].reshape(UNIT, width).astype(jnp.bfloat16)
    part = slice(6 * UNIT, 15 * UNIT)
    ff = out_ref.shape[0]

    def put(columns, total):
        own_ref[:, columns] = total[: 2 * UNIT]
        far_ref[:, columns] = total[2 * UNIT : 3 * UNIT].astype(jnp.bfloat16)
        near_ref[:, columns] = total[3 * UNIT : 5 * UNIT].astype(jnp.bfloat16)
        middle_ref[:, columns] = total[5 * UNIT : 7 * UNIT]
        third_ref[:, columns] = total[7 * UNIT :].astype(jnp.bfloat16)

    step = ff // 2
    for start in range(0, 2 * ff, step):
        columns = slice(start, start + step)
        put(
            columns,
            dot(both_ref[part, :width], in_ref[:, columns]) + dot(twin_ref[part, :width], twin_in_ref[:, columns]),
        )
    for start in range(0, ff, step):
        some = slice(start, start + step)
        put(
            slice(2 * ff + start, 2 * ff + start + step),
            dot(both_ref[part, width:], out_ref[some, :], LAST)
            + dot(twin_ref[part, width:], twin_out_ref[some, :], LAST),
        )


def gateway_kernel(middle_ref, third_ref, far_ref, sum_ref):
    total = middle_ref[...] + third_ref[...].astype(jnp.float32)
    sum_ref[:UNIT, :] = total[:UNIT].astype(jnp.bfloat16)
    sum_ref[UNIT:, :] = (total[UNIT:] + far_ref[...].astype(jnp.float32)).astype(jnp.bfloat16)


def swish_kernel(own_ref, near_ref, passed_ref, twin_near_ref, twin_passed_ref, mid_ref):
    arrived = near_ref[...].astype(jnp.float32) + passed_ref[...].astype(jnp.float32)
    twin = twin_near_ref[...].astype(jnp.float32) + twin_passed_ref[...].astype(jnp.float32)
    share = own_ref[...] + jnp.concatenate(
        [arrived[UNIT:] + twin[:UNIT], arrived[:UNIT] + twin[UNIT:]], axis=0
    )
    ff = share.shape[1] // 3
    gate_part, up_part, back_hidden = share[:, :ff], share[:, ff : 2 * ff], share[:, 2 * ff :]
    sigma = jax.nn.sigmoid(gate_part)
    activated = gate_part * sigma
    slope = sigma + gate_part * sigma * (1.0 - sigma)
    mid_ref[:, :ff] = (activated * up_part).astype(jnp.bfloat16)
    mid_ref[:, ff : 2 * ff] = (back_hidden * up_part * slope).astype(jnp.bfloat16)
    mid_ref[:, 2 * ff :] = (back_hidden * activated).astype(jnp.bfloat16)


def results_kernel(capacity, me_ref, in_ref, out_ref, *refs):
    parts, (back_ref, full_ref) = refs[:-2], refs[-2:]
    at = 0
    for part in parts:
        count = part.shape[0]
        full_ref[at : at + count, :] = part[...]
        at += count
    ff, width = out_ref.shape
    out = dot(full_ref[:, :ff], out_ref[...])
    grad = dot(full_ref[:, ff:], in_ref[...], LAST)
    units = full_ref.shape[0] // UNIT
    blocks = UNIT // capacity
    for k, unit in enumerate(unit_order(me_ref[0], units // 2)):
        here = slice(k * UNIT, (k + 1) * UNIT)
        back_ref[pl.ds(unit * blocks, blocks)] = jnp.concatenate(
            [
                out[here].reshape(blocks, capacity, width),
                grad[here].reshape(blocks, capacity, width),
            ],
            axis=1,
        ).astype(jnp.bfloat16)


def call(kernel, out_shape, flops, *operands, scratch=(), scalar_first=False, in_place=False):
    def size(a):
        return a.size * a.dtype.itemsize

    moved = sum(map(size, operands)) + sum(map(size, jax.tree.leaves(out_shape)))
    space = pl.ANY if in_place else pltpu.VMEM
    specs = [pl.BlockSpec(memory_space=space) for _ in operands]
    if scalar_first:
        specs[0] = pl.BlockSpec(memory_space=pltpu.SMEM)
    return pl.pallas_call(
        kernel,
        out_shape=out_shape,
        in_specs=specs,
        scratch_shapes=scratch,
        compiler_params=pltpu.CompilerParams(vmem_limit_bytes=(60 if in_place else 24) * 2**20),
        cost_estimate=pl.CostEstimate(flops=flops, bytes_accessed=moved, transcendentals=0),
    )(*operands)


def local(tokens, input_weight, output_weight, routes, gates, cotangent):
    block_tok, width = tokens.shape
    route_count = routes.shape[1]
    experts = lax.axis_size("fsdp")
    chips = lax.axis_size("expert") // 2
    ff = output_weight.shape[1]
    capacity = min(block_tok, 2 * block_tok * route_count // experts)
    rows = experts * capacity
    weight_in = input_weight[0]
    weight_out = output_weight[0]
    me = lax.axis_index("expert").reshape(1)
    bf16, f32 = jnp.bfloat16, jnp.float32

    def exchange(values):
        return lax.all_to_all(values, "fsdp", split_axis=0, concat_axis=0, tiled=True)

    def swap(values):
        return lax.ppermute(values, "expert", [(d, d ^ 1) for d in range(2 * chips)])

    def along(values, distance):
        up = [(2 * i, 2 * ((i + distance) % chips)) for i in range(chips)]
        down = [(2 * i + 1, 2 * ((i - distance) % chips) + 1) for i in range(chips)]
        return lax.ppermute(values, "expert", up + down)

    def array(count, columns, dtype):
        return jax.ShapeDtypeStruct((count, columns), dtype)

    sent, maps = call(
        lambda *refs: dispatch_kernel(capacity, *refs),
        (
            jax.ShapeDtypeStruct((experts, 2 * capacity, width), jnp.bfloat16),
            jax.ShapeDtypeStruct((rows, 4 * block_tok), jnp.bfloat16),
        ),
        10 * rows * block_tok * width,
        routes.T,
        gates.T,
        tokens,
        cotangent,
        scratch=[
            pltpu.VMEM((route_count, block_tok), jnp.int32),
            pltpu.VMEM((route_count, block_tok), f32),
            pltpu.VMEM((4 * block_tok, width), bf16),
            pltpu.VMEM((4 * block_tok, width), bf16),
            pltpu.SemaphoreType.DMA((4,)),
        ],
        in_place=True,
    )
    sent, *ready = lax.optimization_barrier((sent, weight_in, weight_out))
    staged = call(
        stage_kernel, (array(width, 2 * ff, bf16), array(ff, width, bf16)), width * ff, *ready
    )
    got, twin_in, twin_out = lax.optimization_barrier((exchange(sent), *map(swap, staged)))
    all_columns = 3 * ff
    routed, own, far, near, middle, third = call(
        lambda *refs: sums_kernel(capacity, *refs),
        (
            array(rows, 2 * width, bf16),
            array(2 * UNIT, all_columns, f32),
            array(UNIT, all_columns, bf16),
            array(2 * UNIT, all_columns, bf16),
            array(2 * UNIT, all_columns, f32),
            array(2 * UNIT, all_columns, bf16),
        ),
        4 * 9 * UNIT * width * all_columns,
        me,
        got,
        swap(got),
        weight_in,
        twin_in,
        weight_out,
        twin_out,
        scratch=[pltpu.VMEM((rows, 2 * width), bf16)],
        scalar_first=True,
    )
    third = along(third, 1)
    far = along(far, 2)
    near = along(near, 1)
    passed = along(
        call(gateway_kernel, array(2 * UNIT, all_columns, bf16), rows * ff, middle, third, far), 2
    )
    chip_mid = call(
        swish_kernel,
        array(2 * UNIT, all_columns, bf16),
        rows * ff,
        own,
        near,
        passed,
        swap(near),
        swap(passed),
    )

    second = along(chip_mid, 2)
    first = along(chip_mid, 1)
    third = along(second, 1)
    far = along(second[:UNIT], 2)
    back, full = call(
        lambda *refs: results_kernel(capacity, *refs),
        (
            jax.ShapeDtypeStruct((experts, 2 * capacity, width), bf16),
            array(rows, all_columns, bf16),
        ),
        2 * rows * width * all_columns,
        me,
        weight_in,
        weight_out,
        first,
        second,
        third,
        chip_mid,
        far,
        swap(first),
        swap(second),
        swap(third),
        swap(far),
        scalar_first=True,
    )
    home = exchange(back)
    hidden, grad_pre = full[:, :ff], full[:, ff:]
    grad_input = dot(routed[:, :width], grad_pre, FIRST).astype(bf16)[None]
    grad_output = dot(hidden, routed[:, width:], FIRST).astype(bf16)[None]
    mixed, grad_tokens = call(
        lambda *refs: combine_kernel(capacity, *refs),
        (
            jax.ShapeDtypeStruct((block_tok, width), jnp.bfloat16),
            jax.ShapeDtypeStruct((block_tok, width), jnp.bfloat16),
        ),
        8 * rows * block_tok * width,
        maps,
        home,
    )
    return (mixed, grad_tokens, grad_input, grad_output)


def solution(mesh):
    placed = (
        P("fsdp", "expert"),
        P("fsdp", "expert", None),
        P("fsdp", None, "expert"),
        P("fsdp", None),
        P("fsdp", None),
        P("fsdp", "expert"),
    )
    return jax.shard_map(
        local,
        mesh=mesh,
        in_specs=placed,
        out_specs=(
            P("fsdp", "expert"),
            P("fsdp", "expert"),
            P("fsdp", "expert", None),
            P("fsdp", None, "expert"),
        ),
        check_vma=False,
    )
```

```python
import jax
import jax.numpy as jnp
from jax import lax
from jax.experimental import pallas as pl
from jax.experimental.pallas import tpu as pltpu
from jax.sharding import PartitionSpec as P

PLAIN = (((1,), (0,)), ((), ()))
LAST = (((1,), (1,)), ((), ()))
FIRST = (((0,), (0,)), ((), ()))
UNIT = 32


def dot(a, b, dims=PLAIN):
    return lax.dot_general(a, b, dims, preferred_element_type=jnp.float32)


def bf16_parts(values):
    first = values.astype(jnp.bfloat16)
    rest = values - first.astype(jnp.float32)
    second = rest.astype(jnp.bfloat16)
    third = (rest - second.astype(jnp.float32)).astype(jnp.bfloat16)
    return first, second, third


def dispatch_kernel(capacity, routes_hbm, gates_hbm, tokens_hbm, cotangent_hbm, sent_ref, maps_ref,
                    routes_ref, gates_ref, tokens_ref, cotangent_ref, arrived):
    experts, _, width = sent_ref.shape
    rows, lanes = maps_ref.shape
    route_count, count = routes_hbm.shape
    copies = [
        pltpu.make_async_copy(source, target, arrived.at[i])
        for i, (source, target) in enumerate(
            (
                (routes_hbm, routes_ref),
                (gates_hbm, gates_ref),
                (tokens_hbm, tokens_ref.at[3 * count : 4 * count]),
                (cotangent_hbm, cotangent_ref.at[3 * count : 4 * count]),
            )
        )
    ]
    for copy in copies:
        copy.start()
    tokens_ref[: 3 * count, :] = jnp.zeros((3 * count, width), jnp.bfloat16)
    cotangent_ref[: 3 * count, :] = jnp.zeros((3 * count, width), jnp.bfloat16)
    token = lax.broadcasted_iota(jnp.int32, (count, lanes), 0)
    lane = lax.broadcasted_iota(jnp.int32, (count, lanes), 1)
    group = [lane == token + i * count for i in range(4)]
    group = [jnp.where(one, 1.0, 0.0).astype(jnp.bfloat16) for one in group]
    first_row = lax.broadcasted_iota(jnp.int32, (rows, experts), 1) * capacity
    at = lax.broadcasted_iota(jnp.int32, (rows, experts), 0)
    inside = (at >= first_row) & (at < first_row + capacity)
    spread = jnp.where(inside, 1.0, 0.0).astype(jnp.bfloat16)
    local_slot = jnp.sum(jnp.where(inside, at - first_row, 0), axis=1, keepdims=True)
    copies[0].wait()
    copies[1].wait()
    everywhere = group[0] + group[1] + group[2] + group[3]
    routes = dot(routes_ref[...].astype(jnp.float32).astype(jnp.bfloat16), everywhere)
    ones = jnp.ones((route_count, count), jnp.bfloat16)
    values = jnp.zeros((route_count, lanes), jnp.float32)
    for part, lanes_of in zip((*bf16_parts(gates_ref[...]), ones), group):
        values = values + dot(part, lanes_of)
    expert = lax.broadcasted_iota(jnp.int32, (experts, lanes), 0).astype(jnp.float32)
    named = jnp.zeros((experts, lanes), jnp.float32)
    value_of = jnp.zeros((experts, lanes), jnp.float32)
    for k in range(route_count):
        hit = routes[k : k + 1, :] == expert
        named = jnp.where(hit, 1.0, named)
        value_of = jnp.where(hit, values[k : k + 1, :], value_of)
    other = lax.broadcasted_iota(jnp.int32, (lanes, lanes), 0)
    mine = lax.broadcasted_iota(jnp.int32, (lanes, lanes), 1)
    for _ in range(3):
        mine = jnp.where(mine >= count, mine - count, mine)
    before = jnp.where(other < mine, 1.0, 0.0).astype(jnp.bfloat16)
    named = named.astype(jnp.bfloat16)
    slot = dot(named, before).astype(jnp.bfloat16)
    picked = (dot(spread, named) > 0.5) & (dot(spread, slot) == local_slot.astype(jnp.float32))
    maps = jnp.where(picked, dot(spread, value_of.astype(jnp.bfloat16)), 0.0)
    is_gate = lax.broadcasted_iota(jnp.int32, (rows, lanes), 1) < 3 * count
    row_gate = jnp.sum(jnp.where(is_gate, maps, 0.0), axis=1, keepdims=True)
    maps = maps.astype(jnp.bfloat16)
    maps_ref[...] = maps
    copies[2].wait()
    copies[3].wait()
    send_rows = dot(maps, tokens_ref[...])
    send_back = row_gate * dot(maps, cotangent_ref[...])
    sent_ref[...] = jnp.concatenate(
        [send_rows.reshape(experts, capacity, width), send_back.reshape(experts, capacity, width)],
        axis=1,
    ).astype(jnp.bfloat16)


def combine_kernel(capacity, maps_ref, home_ref, mixed_ref, grad_ref):
    experts, _, width = home_ref.shape
    count = mixed_ref.shape[0]
    rows = experts * capacity
    home = home_ref[...].astype(jnp.float32)
    out = home[:, :capacity, :].reshape(rows, width).astype(jnp.bfloat16)
    grad = home[:, capacity:, :].reshape(rows, width).astype(jnp.bfloat16)
    total = dot(maps_ref[...], out, FIRST)
    total = total[:count] + total[count : 2 * count] + total[2 * count : 3 * count]
    mixed_ref[...] = total.astype(jnp.bfloat16)
    grad_ref[...] = dot(maps_ref[...], grad, FIRST)[3 * count :].astype(jnp.bfloat16)


def stage_kernel(in_ref, out_ref, staged_in_ref, staged_out_ref):
    staged_in_ref[...] = in_ref[...]
    staged_out_ref[...] = out_ref[...]


def unit_order(me, chips):
    chip, core = lax.div(me, 2), lax.rem(me, 2)
    sign, twin = 1 - 2 * core, 1 - core
    opposite = 2 * lax.rem(chip + 4, chips)
    order = []
    for distance in (1, 2, 3):
        at = 2 * lax.rem(chip - sign * distance + chips, chips)
        order += [at + core, at + twin]
    order += [2 * chip + core, 2 * chip + twin, opposite + core]
    for distance in (1, 2, 3):
        at = 2 * lax.rem(chip + sign * distance + chips, chips)
        order += [at + twin, at + core]
    return order + [opposite + twin]


def sums_kernel(capacity, me_ref, got_ref, twin_got_ref, in_ref, twin_in_ref, out_ref, twin_out_ref,
                both_ref, own_ref, far_ref, near_ref, middle_ref, third_ref, twin_ref):
    experts, _, width = got_ref.shape
    units = both_ref.shape[0] // UNIT
    blocks = UNIT // capacity
    for k, unit in enumerate(unit_order(me_ref[0], units // 2)):
        here = slice(k * UNIT, (k + 1) * UNIT)
        for source, target in ((got_ref, both_ref), (twin_got_ref, twin_ref)):
            block = source[pl.ds(unit * blocks, blocks)].astype(jnp.float32)
            target[here, :width] = block[:, :capacity].reshape(UNIT, width).astype(jnp.bfloat16)
            target[here, width:] = block[:, capacity:].reshape(UNIT, width).astype(jnp.bfloat16)
    part = slice(6 * UNIT, 15 * UNIT)
    ff = out_ref.shape[0]

    def put(columns, total):
        own_ref[:, columns] = total[: 2 * UNIT]
        far_ref[:, columns] = total[2 * UNIT : 3 * UNIT].astype(jnp.bfloat16)
        near_ref[:, columns] = total[3 * UNIT : 5 * UNIT].astype(jnp.bfloat16)
        middle_ref[:, columns] = total[5 * UNIT : 7 * UNIT]
        third_ref[:, columns] = total[7 * UNIT :].astype(jnp.bfloat16)

    step = ff // 2
    for start in range(0, 2 * ff, step):
        columns = slice(start, start + step)
        put(
            columns,
            dot(both_ref[part, :width], in_ref[:, columns]) + dot(twin_ref[part, :width], twin_in_ref[:, columns]),
        )
    for start in range(0, ff, step):
        some = slice(start, start + step)
        put(
            slice(2 * ff + start, 2 * ff + start + step),
            dot(both_ref[part, width:], out_ref[some, :], LAST)
            + dot(twin_ref[part, width:], twin_out_ref[some, :], LAST),
        )


def gateway_kernel(middle_ref, third_ref, far_ref, sum_ref):
    total = middle_ref[...] + third_ref[...].astype(jnp.float32)
    sum_ref[:UNIT, :] = total[:UNIT].astype(jnp.bfloat16)
    sum_ref[UNIT:, :] = (total[UNIT:] + far_ref[...].astype(jnp.float32)).astype(jnp.bfloat16)


def swish_kernel(own_ref, near_ref, passed_ref, twin_near_ref, twin_passed_ref, mid_ref):
    arrived = near_ref[...].astype(jnp.float32) + passed_ref[...].astype(jnp.float32)
    twin = twin_near_ref[...].astype(jnp.float32) + twin_passed_ref[...].astype(jnp.float32)
    share = own_ref[...] + jnp.concatenate(
        [arrived[UNIT:] + twin[:UNIT], arrived[:UNIT] + twin[UNIT:]], axis=0
    )
    ff = share.shape[1] // 3
    gate_part, up_part, back_hidden = share[:, :ff], share[:, ff : 2 * ff], share[:, 2 * ff :]
    sigma = jax.nn.sigmoid(gate_part)
    activated = gate_part * sigma
    slope = sigma + gate_part * sigma * (1.0 - sigma)
    mid_ref[:, :ff] = (activated * up_part).astype(jnp.bfloat16)
    mid_ref[:, ff : 2 * ff] = (back_hidden * up_part * slope).astype(jnp.bfloat16)
    mid_ref[:, 2 * ff :] = (back_hidden * activated).astype(jnp.bfloat16)


def results_kernel(capacity, me_ref, in_ref, out_ref, *refs):
    parts, (back_ref, full_ref) = refs[:-2], refs[-2:]
    at = 0
    for part in parts:
        count = part.shape[0]
        full_ref[at : at + count, :] = part[...]
        at += count
    ff, width = out_ref.shape
    out = dot(full_ref[:, :ff], out_ref[...])
    grad = dot(full_ref[:, ff:], in_ref[...], LAST)
    units = full_ref.shape[0] // UNIT
    blocks = UNIT // capacity
    for k, unit in enumerate(unit_order(me_ref[0], units // 2)):
        here = slice(k * UNIT, (k + 1) * UNIT)
        back_ref[pl.ds(unit * blocks, blocks)] = jnp.concatenate(
            [
                out[here].reshape(blocks, capacity, width),
                grad[here].reshape(blocks, capacity, width),
            ],
            axis=1,
        ).astype(jnp.bfloat16)


def call(kernel, out_shape, flops, *operands, scratch=(), scalar_first=False, in_place=False):
    def size(a):
        return a.size * a.dtype.itemsize

    moved = sum(map(size, operands)) + sum(map(size, jax.tree.leaves(out_shape)))
    space = pl.ANY if in_place else pltpu.VMEM
    specs = [pl.BlockSpec(memory_space=space) for _ in operands]
    if scalar_first:
        specs[0] = pl.BlockSpec(memory_space=pltpu.SMEM)
    return pl.pallas_call(
        kernel,
        out_shape=out_shape,
        in_specs=specs,
        scratch_shapes=scratch,
        compiler_params=pltpu.CompilerParams(vmem_limit_bytes=(60 if in_place else 24) * 2**20),
        cost_estimate=pl.CostEstimate(flops=flops, bytes_accessed=moved, transcendentals=0),
    )(*operands)


def local(tokens, input_weight, output_weight, routes, gates, cotangent):
    block_tok, width = tokens.shape
    route_count = routes.shape[1]
    experts = lax.axis_size("fsdp")
    chips = lax.axis_size("expert") // 2
    ff = output_weight.shape[1]
    capacity = min(block_tok, 2 * block_tok * route_count // experts)
    rows = experts * capacity
    weight_in = input_weight[0]
    weight_out = output_weight[0]
    me = lax.axis_index("expert").reshape(1)
    bf16, f32 = jnp.bfloat16, jnp.float32

    def exchange(values):
        return lax.all_to_all(values, "fsdp", split_axis=0, concat_axis=0, tiled=True)

    def swap(values):
        return lax.ppermute(values, "expert", [(d, d ^ 1) for d in range(2 * chips)])

    def along(values, distance):
        up = [(2 * i, 2 * ((i + distance) % chips)) for i in range(chips)]
        down = [(2 * i + 1, 2 * ((i - distance) % chips) + 1) for i in range(chips)]
        return lax.ppermute(values, "expert", up + down)

    def array(count, columns, dtype):
        return jax.ShapeDtypeStruct((count, columns), dtype)

    sent, maps = call(
        lambda *refs: dispatch_kernel(capacity, *refs),
        (
            jax.ShapeDtypeStruct((experts, 2 * capacity, width), jnp.bfloat16),
            jax.ShapeDtypeStruct((rows, 4 * block_tok), jnp.bfloat16),
        ),
        10 * rows * block_tok * width,
        routes.T,
        gates.T,
        tokens,
        cotangent,
        scratch=[
            pltpu.VMEM((route_count, block_tok), jnp.int32),
            pltpu.VMEM((route_count, block_tok), f32),
            pltpu.VMEM((4 * block_tok, width), bf16),
            pltpu.VMEM((4 * block_tok, width), bf16),
            pltpu.SemaphoreType.DMA((4,)),
        ],
        in_place=True,
    )
    sent, *ready = lax.optimization_barrier((sent, weight_in, weight_out))
    staged = call(
        stage_kernel, (array(width, 2 * ff, bf16), array(ff, width, bf16)), width * ff, *ready
    )
    got, twin_in, twin_out = lax.optimization_barrier((exchange(sent), *map(swap, staged)))
    all_columns = 3 * ff
    routed, own, far, near, middle, third = call(
        lambda *refs: sums_kernel(capacity, *refs),
        (
            array(rows, 2 * width, bf16),
            array(2 * UNIT, all_columns, f32),
            array(UNIT, all_columns, bf16),
            array(2 * UNIT, all_columns, bf16),
            array(2 * UNIT, all_columns, f32),
            array(2 * UNIT, all_columns, bf16),
        ),
        4 * 9 * UNIT * width * all_columns,
        me,
        got,
        swap(got),
        weight_in,
        twin_in,
        weight_out,
        twin_out,
        scratch=[pltpu.VMEM((rows, 2 * width), bf16)],
        scalar_first=True,
    )
    third = along(third, 1)
    far = along(far, 2)
    near = along(near, 1)
    passed = along(
        call(gateway_kernel, array(2 * UNIT, all_columns, bf16), rows * ff, middle, third, far), 2
    )
    chip_mid = call(
        swish_kernel,
        array(2 * UNIT, all_columns, bf16),
        rows * ff,
        own,
        near,
        passed,
        swap(near),
        swap(passed),
    )

    second = along(chip_mid, 2)
    first = along(chip_mid, 1)
    third = along(second, 1)
    far = along(third[:UNIT], 1)
    back, full = call(
        lambda *refs: results_kernel(capacity, *refs),
        (
            jax.ShapeDtypeStruct((experts, 2 * capacity, width), bf16),
            array(rows, all_columns, bf16),
        ),
        2 * rows * width * all_columns,
        me,
        weight_in,
        weight_out,
        first,
        second,
        third,
        chip_mid,
        far,
        swap(first),
        swap(second),
        swap(third),
        swap(far),
        scalar_first=True,
    )
    home = exchange(back)
    hidden, grad_pre = full[:, :ff], full[:, ff:]
    grad_input = dot(routed[:, :width], grad_pre, FIRST).astype(bf16)[None]
    grad_output = dot(hidden, routed[:, width:], FIRST).astype(bf16)[None]
    mixed, grad_tokens = call(
        lambda *refs: combine_kernel(capacity, *refs),
        (
            jax.ShapeDtypeStruct((block_tok, width), jnp.bfloat16),
            jax.ShapeDtypeStruct((block_tok, width), jnp.bfloat16),
        ),
        8 * rows * block_tok * width,
        maps,
        home,
    )
    return (mixed, grad_tokens, grad_input, grad_output)


def solution(mesh):
    placed = (
        P("fsdp", "expert"),
        P("fsdp", "expert", None),
        P("fsdp", None, "expert"),
        P("fsdp", None),
        P("fsdp", None),
        P("fsdp", "expert"),
    )
    return jax.shard_map(
        local,
        mesh=mesh,
        in_specs=placed,
        out_specs=(
            P("fsdp", "expert"),
            P("fsdp", "expert"),
            P("fsdp", "expert", None),
            P("fsdp", None, "expert"),
        ),
        check_vma=False,
    )
```
